512 devices in a mesh: dp: 32 (over y, x), tensor: 16 (over z, core).
Axes of the slice: x: 4, y: 8, z: 8, core: 2. Of those that a mesh axis runs over, the one named last changes fastest.
Arguments:
- hidden_in: bfloat16 [2048, 12288], P('dp'), may hold values from -6 to 6
- norm_gain: bfloat16 [12288], replicated, may hold values from 0.099609375 to 1.8984375
- norm_shift: bfloat16 [12288], replicated, may hold values from -3 to 3
- up_weight: bfloat16 [12288, 24576], P('dp', 'tensor'), may hold values from -0.0546875 to 0.0546875
- up_bias: bfloat16 [24576], P('tensor'), may hold values from -3 to 3
- down_weight: bfloat16 [24576, 12288], P('tensor', 'dp'), may hold values from -0.09375 to 0.09375
- down_bias: bfloat16 [12288], P('tensor'), may hold values from -3 to 3
- active: int32 [64, 16, 4], P(None, 'tensor'), may hold values from 0 to 11, as said below
- counts: int32 [64, 16], P(None, 'tensor'), may hold values from 1 to 4, as said below
Outputs:
- hidden_out: bfloat16 [2048, 12288], P('dp', 'tensor')
The draws below stay inside these ranges and needn't reach their ends.
Inputs may be any that keep to these rules, and one draw needn't show every extreme that they name: The 4 entries of each list are distinct; only the first counts entries are active. `counts`: every row group has a list with all 4 slots valid.
All inputs are finite; a program needn't handle non-finite values.
Results may differ from the reference program's by a relative error of at most 0.022.
Values may be sent and summed in bfloat16 or wider, within the bound.
No kernel may reach another device: no remote copies, remote signals or barrier semaphores. Data moves between devices by JAX's collectives and lax.ppermute only.
A program may use at most 64 MiB of HBM per device.

```python
import jax
import jax.numpy as jnp
from jax import lax

D = 12288
FFW = 24576
BLOCK = 128
CAP = 4
GROUP = 32
ROWS = 2048
GROUPS = 64
OWNERS = 16
N_DP = 32


def draw_lists(key):
    first = jax.random.fold_in(key, 11)
    second = jax.random.fold_in(key, 12)
    own = FFW // BLOCK // OWNERS
    keys = jax.random.split(first, GROUPS * OWNERS)
    ids = jax.vmap(lambda single: jax.random.permutation(single, own)[:CAP])(keys)
    ids = ids.reshape(GROUPS, OWNERS, CAP).astype(jnp.int32)
    valid = jax.random.randint(second, (GROUPS, OWNERS), 1, CAP + 1)
    full = jnp.arange(OWNERS)[None, :] == (jnp.arange(GROUPS) % OWNERS)[:, None]
    valid = jnp.where(full, CAP, valid).astype(jnp.int32)
    return (ids, valid)


def draw_active(key, part):
    return draw_lists(key)[0]


def draw_counts(key, part):
    return draw_lists(key)[1]


def shard_levels(key, extent, pieces, smallest, top_value):
    level = 1.0
    for axis_at, shards_of in pieces:
        steps = jax.random.uniform(jax.random.fold_in(jax.random.fold_in(key, 6), axis_at), (shards_of,), jnp.float32, smallest / len(pieces), top_value / len(pieces))
        level = level * jnp.repeat(jnp.exp(steps), extent[axis_at] // shards_of).reshape((-1,) + (1,) * (len(extent) - 1 - axis_at))
    return level


def scatter_about(key, shape, scale, bound, cuts=(), kind=jnp.bfloat16):
    gain = shard_levels(key, shape, cuts, -0.22, 0.18) if cuts else 1.0
    array = jax.random.normal(key, shape, jnp.float32) * scale * gain
    return jnp.minimum(jnp.maximum(array, -bound), bound).astype(kind)


def setup_inputs(seed: int = 0) -> dict:
    streams_of = jax.random.split(jax.random.key(seed), 10)
    return {
        "hidden_in": scatter_about(streams_of[0], (ROWS, D), 1.0, 6.0, ((0, 32),)),
        "norm_gain": jnp.clip(1.0 + 0.18 * jax.random.normal(streams_of[1], (D,), jnp.float32), 0.099609375, 1.8984375).astype(jnp.bfloat16),
        "norm_shift": scatter_about(streams_of[2], (D,), 0.4, 3.0),
        "up_weight": scatter_about(streams_of[3], (D, FFW), D ** -0.5, 0.0546875, ((0, 32), (1, 16))),
        "up_bias": scatter_about(streams_of[4], (FFW,), 0.5, 3.0, ((0, 16),)),
        "down_weight": scatter_about(streams_of[5], (FFW, D), (FFW // 6) ** -0.5, 0.09375, ((0, 16), (1, 32))),
        "down_bias": scatter_about(streams_of[6], (D,), 0.5, 3.0, ((0, 16),)),
        "active": draw_active(jax.random.fold_in(streams_of[9], 71), 0),
        "counts": draw_counts(jax.random.fold_in(streams_of[9], 71), 0),
    }


def reference(hidden_in, norm_gain, norm_shift, up_weight, up_bias, down_weight, down_bias, active, counts):
    d_part = D // N_DP
    own = FFW // BLOCK // OWNERS
    values = hidden_in.astype(jnp.float32)
    center = values - lax.optimization_barrier(jnp.mean(values, axis=-1, keepdims=True))
    spread = lax.optimization_barrier(jnp.mean(center * center, axis=-1, keepdims=True))
    normed = (center * lax.rsqrt(spread + 1e-05) * norm_gain.astype(jnp.float32) + norm_shift.astype(jnp.float32)).astype(jnp.bfloat16)
    up_table = up_weight.reshape(N_DP, d_part, OWNERS, own, BLOCK)
    down_table = down_weight.reshape(OWNERS, own, BLOCK, N_DP, d_part)
    bias_table = up_bias.astype(jnp.float32).reshape(OWNERS, own, BLOCK)
    owner_ids = jnp.arange(OWNERS, dtype=jnp.int32)[:, None]
    slot_ids = jnp.arange(CAP, dtype=jnp.int32)[None, :]
    grouped = normed.reshape(GROUPS, GROUP, N_DP, d_part)

    def one_group(items):
        rows, ids, valid = items
        chosen_up = up_table[:, :, owner_ids, ids]
        part = jnp.einsum('rpd,pdocb->rpocb', rows.astype(jnp.float32), chosen_up.astype(jnp.float32))
        part = lax.optimization_barrier(part.astype(jnp.bfloat16))
        pre = lax.optimization_barrier(jnp.sum(part.astype(jnp.float32), axis=1))
        bias_sel = bias_table[owner_ids, ids]
        mask = (slot_ids < valid[:, None]).astype(jnp.float32)
        act = (jnp.maximum(pre + bias_sel[None], 0.0) * mask[None, :, :, None]).astype(jnp.bfloat16)
        chosen_down = down_table[owner_ids, ids]
        branch = jnp.einsum('rocb,ocbpd->ropd', act.astype(jnp.float32), chosen_down.astype(jnp.float32))
        branch = lax.optimization_barrier(branch.astype(jnp.bfloat16))
        return lax.optimization_barrier(jnp.sum(branch.astype(jnp.float32), axis=1)).reshape(GROUP, D)
    total = lax.map(one_group, (grouped, active, counts)).reshape(ROWS, D)
    return (values + total + down_bias.astype(jnp.float32)).astype(jnp.bfloat16)
```

```python
import functools

import jax
import jax.numpy as jnp
from jax import lax
from jax.experimental import pallas as pl
from jax.experimental.pallas import tpu as pltpu
from jax.sharding import Mesh, PartitionSpec as P

BLOCK = 128
GROUP = 32
CAP = 4
NY, NX, NZ, NC = 8, 4, 8, 2
ROW = 64
PIECE = 384
F32 = jnp.float32
BF16 = jnp.bfloat16
ALL = ("y", "x", "z", "c")


def around(size, k):
    return [(i, (i + k) % size) for i in range(size)]


def up_kernel(where, ids, own, other, weight, out, rows, total):
    step = pl.program_id(0)
    c = where[1]
    half = own.shape[1]
    rows[pl.ds(pl.multiple_of(c * half, half), half), :] = own[0]
    rows[pl.ds(pl.multiple_of((1 - c) * half, half), half), :] = other[0]
    total[...] = jnp.dot(rows[...], weight[...], preferred_element_type=F32)
    groups = 2 * half // GROUP
    for g in range(groups):
        for s in range(CAP):
            block = ids[step * groups + g, s]
            picked = total[
                g * GROUP : (g + 1) * GROUP, pl.ds(pl.multiple_of(block * BLOCK, BLOCK), BLOCK)
            ]
            out[g // 2, 0, (g % 2) * GROUP : (g % 2 + 1) * GROUP, s * BLOCK : (s + 1) * BLOCK] = (
                picked.astype(BF16)
            )


def up(where, ids, own, other, weight):
    half = own.shape[1]
    return pl.pallas_call(
        up_kernel,
        out_shape=jax.ShapeDtypeStruct((NX, NY, ROW, CAP * BLOCK), BF16),
        grid_spec=pltpu.PrefetchScalarGridSpec(
            num_scalar_prefetch=2,
            grid=(NY,),
            in_specs=[
                pl.BlockSpec((1, half, PIECE), lambda i, *_: (i, 0, 0)),
                pl.BlockSpec((1, half, PIECE), lambda i, *_: (i, 0, 0)),
                pl.BlockSpec(weight.shape, lambda i, *_: (0, 0)),
            ],
            out_specs=pl.BlockSpec((NX, 1, ROW, CAP * BLOCK), lambda i, *_: (0, i, 0, 0)),
            scratch_shapes=[
                pltpu.VMEM((2 * half, PIECE), BF16),
                pltpu.VMEM((2 * half, weight.shape[1]), F32),
            ],
        ),
        compiler_params=pltpu.CompilerParams(vmem_limit_bytes=32 * 2**20),
        name="up",
    )(where, ids, own, other, weight)


def act_kernel(where, ids, valid, parts, bias, out):
    pre = jnp.sum(parts[...].astype(F32), axis=0)
    for g in range(ROW // GROUP):
        group = where[0] * (ROW // GROUP) + g
        for s in range(CAP):
            block = ids[group, s]
            keep = (s < valid[group]).astype(F32)
            mine = pre[g * GROUP : (g + 1) * GROUP, s * BLOCK : (s + 1) * BLOCK]
            value = jnp.maximum(mine + bias[pl.ds(block, 1), :], 0.0) * keep
            out[g * GROUP : (g + 1) * GROUP, s * BLOCK : (s + 1) * BLOCK] = value.astype(BF16)


def activate(where, ids, valid, parts, bias):
    smem = pl.BlockSpec(memory_space=pltpu.SMEM)
    vmem = pl.BlockSpec(memory_space=pltpu.VMEM)
    return pl.pallas_call(
        act_kernel,
        out_shape=jax.ShapeDtypeStruct((ROW, CAP * BLOCK), BF16),
        in_specs=[smem, smem, smem, vmem, vmem],
        out_specs=vmem,
        compiler_params=pltpu.CompilerParams(vmem_limit_bytes=32 * 2**20),
        name="act",
    )(where, ids, valid, parts, bias)


def down_kernel(where, ids, a0, a1, a2, a3, weight, keep, send, wide):
    step = pl.program_id(0)
    x, c = where[2], where[1]
    wide[...] = jnp.zeros_like(wide)
    for k, ref in enumerate((a0, a1, a2, a3)):
        source = lax.rem(x + NX - k, NX)
        for g in range(ROW // GROUP):
            group = (step * NX + source) * (ROW // GROUP) + g
            at = pl.multiple_of(source * ROW + g * GROUP, GROUP)
            for s in range(CAP):
                block = ids[group, s]
                wide[pl.ds(at, GROUP), pl.ds(pl.multiple_of(block * BLOCK, BLOCK), BLOCK)] = ref[
                    0, g * GROUP : (g + 1) * GROUP, s * BLOCK : (s + 1) * BLOCK
                ]
    half = keep.shape[1]
    for ref, part in ((keep, c), (send, 1 - c)):
        rows = wide[pl.ds(pl.multiple_of(part * half, half), half), :]
        ref[0] = jnp.dot(rows, weight[...], preferred_element_type=F32).astype(BF16)


def down(where, ids, acts, weight):
    half = NX * ROW // 2
    spec = pl.BlockSpec((1, ROW, CAP * BLOCK), lambda i, *_: (i, 0, 0))
    out_spec = pl.BlockSpec((1, half, PIECE), lambda i, *_: (i, 0, 0))
    return pl.pallas_call(
        down_kernel,
        out_shape=[jax.ShapeDtypeStruct((NY, half, PIECE), BF16)] * 2,
        grid_spec=pltpu.PrefetchScalarGridSpec(
            num_scalar_prefetch=2,
            grid=(NY,),
            in_specs=[spec] * 4 + [pl.BlockSpec(weight.shape, lambda i, *_: (0, 0))],
            out_specs=[out_spec, out_spec],
            scratch_shapes=[pltpu.VMEM((2 * half, weight.shape[0]), BF16)],
        ),
        compiler_params=pltpu.CompilerParams(vmem_limit_bytes=32 * 2**20),
        name="down",
    )(where, ids, *acts, weight)


def body(
    hidden_in, norm_gain, norm_shift, up_weight, up_bias, down_weight, down_bias, active, counts
):
    y, x = lax.axis_index("y"), lax.axis_index("x")
    z, c = lax.axis_index("z"), lax.axis_index("c")
    r, t = y * NX + x, z * NC + c
    odd = lax.rem(r, 2) == 1
    ids, valid = active[:, 0, :], counts[:, 0]
    where = jnp.stack([r, c, x]).astype(jnp.int32)
    width = down_bias.shape[0]

    values = hidden_in.astype(F32)
    mean = jnp.mean(values, axis=-1, keepdims=True)
    center = values - mean
    spread = jnp.mean(center * center, axis=-1, keepdims=True)
    mine = lax.dynamic_slice_in_dim(hidden_in, t * width, width, 1).astype(F32)
    gain = lax.dynamic_slice_in_dim(norm_gain, t * width, width, 0).astype(F32)
    shift = lax.dynamic_slice_in_dim(norm_shift, t * width, width, 0).astype(F32)
    normed = ((mine - mean) * lax.rsqrt(spread + 1e-05) * gain + shift).astype(BF16)

    there = [
        [
            (p * 16 + q, (2 * q + (j ^ (p & 1))) * 16 + p // 2)
            for p in range(32)
            for q in range(16)
        ]
        for j in range(2)
    ]
    back = [
        [
            (p * 16 + q, (2 * q + (j ^ (p & 1))) * 16 + p // 2)
            for p in range(32)
            for q in range(16)
        ]
        for j in range(2)
    ]
    low, high = normed[:, :PIECE], normed[:, PIECE:]
    first = lax.ppermute(jnp.where(odd, high, low), ALL, there[0])
    second = lax.ppermute(jnp.where(odd, low, high), ALL, there[1])
    rows = jnp.concatenate(
        [jnp.where(odd, second, first), jnp.where(odd, first, second)], axis=0
    )
    own = lax.all_gather(rows, "z", axis=0, tiled=False)
    other = lax.ppermute(own, "c", around(NC, 1))

    part = up(where, ids, own, other, up_weight)
    part = lax.all_to_all(part, "x", split_axis=0, concat_axis=0, tiled=True)
    part = jnp.sum(part.astype(F32), axis=0).astype(BF16)
    part = lax.all_to_all(part, "y", split_axis=0, concat_axis=0, tiled=True)
    bias = up_bias.astype(F32).reshape(-1, BLOCK)
    act = activate(where, ids, valid, part, bias)

    act = lax.all_gather(act, "y", axis=0, tiled=False)
    acts = [act] + [lax.ppermute(act, "x", around(NX, k)) for k in range(1, NX)]
    keep, send = down(where, ids, acts, down_weight)
    got = lax.ppermute(send, "c", around(NC, 1))
    pair = (keep.astype(F32) + got.astype(F32)).astype(BF16)
    pair = lax.all_to_all(pair, "z", split_axis=0, concat_axis=0, tiled=True)
    branch = jnp.sum(pair.astype(F32), axis=0).astype(BF16)

    low, high = branch[:ROW], branch[ROW:]
    first = lax.ppermute(jnp.where(odd, high, low), ALL, back[0])
    second = lax.ppermute(jnp.where(odd, low, high), ALL, back[1])
    summed = jnp.concatenate(
        [jnp.where(odd, second, first), jnp.where(odd, first, second)], axis=1
    ).astype(F32)
    resid = lax.dynamic_slice_in_dim(hidden_in, t * width, width, 1).astype(F32)
    return (resid + summed + down_bias.astype(F32)).astype(BF16)


def solution(mesh):
    fine = Mesh(mesh.devices.reshape(NY, NX, NZ, NC), ALL)
    dp, tensor = ("y", "x"), ("z", "c")
    placed = (
        P(dp, None),
        P(),
        P(),
        P(dp, tensor),
        P(tensor),
        P(tensor, dp),
        P(tensor),
        P(None, tensor, None),
        P(None, tensor),
    )
    return jax.shard_map(
        body, mesh=fine, in_specs=placed, out_specs=P(dp, tensor), check_vma=False
    )
```

```python
import jax
import jax.numpy as jnp
from jax import lax
from jax.experimental import pallas as pl
from jax.experimental.pallas import tpu as pltpu
from jax.sharding import Mesh, PartitionSpec as P

BLOCK = 128
GROUP = 32
CAP = 4
NY, NX, NZ, NC = 8, 4, 8, 2
ROW = 64
PIECE = 384
F32 = jnp.float32
BF16 = jnp.bfloat16
ALL = ("y", "x", "z", "c")


def around(size, k):
    return [(i, (i + k) % size) for i in range(size)]


def norm_kernel(half, hidden, gain, shift, out):
    rows, features = hidden.shape
    pieces = features // PIECE

    def piece(p):
        return hidden[:, p * PIECE : (p + 1) * PIECE].astype(F32)

    total = jnp.zeros((rows, PIECE), F32)
    for p in range(pieces):
        total += piece(p)
    mean = jnp.sum(total, axis=1, keepdims=True) / features
    total = jnp.zeros((rows, PIECE), F32)
    for p in range(pieces):
        center = piece(p) - mean
        total += center * center
    spread = jnp.sum(total, axis=1, keepdims=True) / features
    scale = lax.rsqrt(spread + 1e-05)
    for p in range(pieces):
        value = (piece(p) - mean) * scale * gain[p : p + 1, :] + shift[p : p + 1, :]
        out[p] = value.astype(BF16)


def norm(half, hidden, gain, shift):
    features = hidden.shape[1]
    pieces = features // PIECE
    return pl.pallas_call(
        norm_kernel,
        out_shape=jax.ShapeDtypeStruct((pieces, GROUP, PIECE), BF16),
        grid_spec=pltpu.PrefetchScalarGridSpec(
            num_scalar_prefetch=1,
            grid=(1,),
            in_specs=[
                pl.BlockSpec((GROUP, features), lambda i, half: (half[0], 0)),
                pl.BlockSpec((pieces, PIECE), lambda i, half: (0, 0)),
                pl.BlockSpec((pieces, PIECE), lambda i, half: (0, 0)),
            ],
            out_specs=pl.BlockSpec((pieces, GROUP, PIECE), lambda i, half: (0, 0, 0)),
        ),
        compiler_params=pltpu.CompilerParams(vmem_limit_bytes=32 * 2**20),
        name="norm",
    )(half, hidden, gain, shift)


SMEM = pl.BlockSpec(memory_space=pltpu.SMEM)
VMEM = pl.BlockSpec(memory_space=pltpu.VMEM)
TOGETHER = 8


def up_kernel(half, ids, rows, weight, *rest):
    out, total = rest[-2:]
    h = half[0]
    for first in range(0, NY * NX, TOGETHER):
        block_rows = rows[first : first + TOGETHER].reshape(TOGETHER * GROUP, PIECE)
        total[...] = jnp.dot(block_rows, weight[...], preferred_element_type=F32)
        for i in range(TOGETHER):
            r = first + i
            for s in range(CAP):
                at = pl.multiple_of(ids[2 * r + h, s] * BLOCK, BLOCK)
                picked = total[i * GROUP : (i + 1) * GROUP, pl.ds(at, BLOCK)]
                out[r % NX, r // NX, h, :, s * BLOCK : (s + 1) * BLOCK] = picked.astype(BF16)


def up(half, ids, rows, weight, before=None):
    shape = (NX, NY, ROW // GROUP, GROUP, CAP * BLOCK)
    more = () if before is None else (before,)
    return pl.pallas_call(
        up_kernel,
        out_shape=jax.ShapeDtypeStruct(shape, BF16),
        in_specs=[SMEM, SMEM, VMEM, VMEM] + [VMEM] * len(more),
        out_specs=VMEM,
        scratch_shapes=[pltpu.VMEM((TOGETHER * GROUP, weight.shape[1]), F32)],
        input_output_aliases={4: 0} if more else {},
        compiler_params=pltpu.CompilerParams(vmem_limit_bytes=24 * 2**20),
        name="up_second" if more else "up_first",
    )(half, ids, rows, weight, *more)


def act_kernel(where, ids, valid, parts, bias, out):
    pre = jnp.sum(parts[...].astype(F32), axis=0)
    for g in range(ROW // GROUP):
        group = where[0] * (ROW // GROUP) + g
        for s in range(CAP):
            block = ids[group, s]
            keep = (s < valid[group]).astype(F32)
            mine = pre[g * GROUP : (g + 1) * GROUP, s * BLOCK : (s + 1) * BLOCK]
            value = (jnp.maximum(mine + bias[pl.ds(block, 1), :], 0.0) * keep).astype(BF16)
            for copy in range(out.shape[0]):
                out[copy, g * GROUP : (g + 1) * GROUP, s * BLOCK : (s + 1) * BLOCK] = value


def activate(where, ids, valid, parts, bias):
    return pl.pallas_call(
        act_kernel,
        out_shape=jax.ShapeDtypeStruct((NY, ROW, CAP * BLOCK), BF16),
        in_specs=[SMEM, SMEM, SMEM, VMEM, VMEM],
        out_specs=VMEM,
        compiler_params=pltpu.CompilerParams(vmem_limit_bytes=24 * 2**20),
        name="act",
    )(where, ids, valid, parts, bias)


def down_kernel(where, ids, a0, a1, a2, a3, weight, keep, send, wide):
    x, c = where[2], where[1]
    for k, ref in enumerate((a0, a1, a2, a3)):
        source = lax.rem(x + NX - k, NX)
        wide[...] = jnp.zeros_like(wide)
        for y in range(NY):
            for g in range(ROW // GROUP):
                group = (y * NX + source) * (ROW // GROUP) + g
                low = y * ROW + g * GROUP
                for s in range(CAP):
                    at = pl.multiple_of(ids[group, s] * BLOCK, BLOCK)
                    wide[low : low + GROUP, pl.ds(at, BLOCK)] = ref[
                        y, g * GROUP : (g + 1) * GROUP, s * BLOCK : (s + 1) * BLOCK
                    ]
        value = jnp.dot(wide[...], weight[...], preferred_element_type=F32).astype(BF16)
        value = value.reshape(NY, ROW, PIECE)
        own, part = source // 2 == c, lax.rem(source, 2)

        @pl.when(own)
        def _():
            keep[:, part] = value

        @pl.when(jnp.logical_not(own))
        def _():
            send[:, part] = value


def down(where, ids, acts, weight):
    return pl.pallas_call(
        down_kernel,
        out_shape=[jax.ShapeDtypeStruct((NY, 2, ROW, PIECE), BF16)] * 2,
        in_specs=[SMEM, SMEM] + [VMEM] * 5,
        out_specs=[VMEM, VMEM],
        scratch_shapes=[pltpu.VMEM((NY * ROW, weight.shape[0]), BF16)],
        compiler_params=pltpu.CompilerParams(vmem_limit_bytes=24 * 2**20),
        name="down",
    )(where, ids, *acts, weight)


def body(
    hidden_in, norm_gain, norm_shift, up_weight, up_bias, down_weight, down_bias, active, counts
):
    y, x = lax.axis_index("y"), lax.axis_index("x")
    z, c = lax.axis_index("z"), lax.axis_index("c")
    r, t = y * NX + x, z * NC + c
    odd = lax.rem(r, 2) == 1
    ids, valid = active[:, 0, :], counts[:, 0]
    where = jnp.stack([r, c, x]).astype(jnp.int32)
    width = down_bias.shape[0]

    mine, others = c.reshape(1), (1 - c).reshape(1)
    gain = norm_gain.astype(F32).reshape(-1, PIECE)
    shift = norm_shift.astype(F32).reshape(-1, PIECE)
    normed = norm(mine, hidden_in, gain, shift)
    own = lax.all_to_all(normed, ("y", "x"), split_axis=0, concat_axis=0, tiled=True)
    other = lax.ppermute(own, "c", around(NC, 1))
    part = up(mine, ids, own, up_weight)
    part = up(others, ids, other, up_weight, part).reshape(NX, NY, ROW, CAP * BLOCK)
    part = lax.all_to_all(part, "x", split_axis=0, concat_axis=0, tiled=True)
    part = jnp.sum(part.astype(F32), axis=0).astype(BF16)
    part = lax.all_to_all(part, "y", split_axis=0, concat_axis=0, tiled=True)
    bias = up_bias.astype(F32).reshape(-1, BLOCK)
    act = activate(where, ids, valid, part, bias)

    act = lax.all_to_all(act, "y", split_axis=0, concat_axis=0, tiled=True)
    acts = [act] + [lax.ppermute(act, "x", around(NX, k)) for k in range(1, NX)]
    keep, send = down(where, ids, acts, down_weight)
    got = lax.ppermute(send, "c", around(NC, 1))
    pair = (keep.astype(F32) + got.astype(F32)).astype(BF16).reshape(NZ, 2 * ROW, PIECE)
    pair = lax.all_to_all(pair, "z", split_axis=0, concat_axis=0, tiled=True)
    branch = jnp.sum(pair.astype(F32), axis=0).astype(BF16)

    back = [
        [
            (p * 16 + q, (2 * q + (j ^ (p & 1))) * 16 + p // 2)
            for p in range(32)
            for q in range(16)
        ]
        for j in range(2)
    ]
    low, high = branch[:ROW], branch[ROW:]
    first = lax.ppermute(jnp.where(odd, high, low), ALL, back[0])
    second = lax.ppermute(jnp.where(odd, low, high), ALL, back[1])
    summed = jnp.concatenate(
        [jnp.where(odd, second, first), jnp.where(odd, first, second)], axis=1
    ).astype(F32)
    resid = lax.dynamic_slice_in_dim(hidden_in, t * width, width, 1).astype(F32)
    return (resid + summed + down_bias.astype(F32)).astype(BF16)


def solution(mesh):
    fine = Mesh(mesh.devices.reshape(NY, NX, NZ, NC), ALL)
    dp, tensor = ("y", "x"), ("z", "c")
    placed = (
        P(dp, None),
        P(),
        P(),
        P(dp, tensor),
        P(tensor),
        P(tensor, dp),
        P(tensor),
        P(None, tensor, None),
        P(None, tensor),
    )
    return jax.shard_map(
        body, mesh=fine, in_specs=placed, out_specs=P(dp, tensor), check_vma=False
    )
```

```python
import functools

import jax
import jax.numpy as jnp
from jax import lax
from jax.experimental import pallas as pl
from jax.experimental.pallas import tpu as pltpu
from jax.sharding import Mesh, PartitionSpec as P

BLOCK = 128
GROUP = 32
CAP = 4
NY, NX, NZ, NC = 8, 4, 8, 2
ROW = 64
PIECE = 384
F32 = jnp.float32
BF16 = jnp.bfloat16
ALL = ("y", "x", "z", "c")


def around(size, k):
    return [(i, (i + k) % size) for i in range(size)]


def norm_kernel(half, hidden, gain, shift, out):
    rows, features = hidden.shape
    pieces = features // PIECE

    def piece(p):
        return hidden[:, p * PIECE : (p + 1) * PIECE].astype(F32)

    total = jnp.zeros((rows, PIECE), F32)
    for p in range(pieces):
        total += piece(p)
    mean = jnp.sum(total, axis=1, keepdims=True) / features
    total = jnp.zeros((rows, PIECE), F32)
    for p in range(pieces):
        center = piece(p) - mean
        total += center * center
    spread = jnp.sum(total, axis=1, keepdims=True) / features
    scale = lax.rsqrt(spread + 1e-05)
    for p in range(pieces):
        at = slice(p * PIECE, (p + 1) * PIECE)
        value = (piece(p) - mean) * scale * gain[:, at].astype(F32) + shift[:, at].astype(F32)
        out[p] = value.astype(BF16)


def norm(half, hidden, gain, shift):
    features = hidden.shape[1]
    pieces = features // PIECE
    return pl.pallas_call(
        norm_kernel,
        out_shape=jax.ShapeDtypeStruct((pieces, GROUP, PIECE), BF16),
        grid_spec=pltpu.PrefetchScalarGridSpec(
            num_scalar_prefetch=1,
            grid=(1,),
            in_specs=[
                pl.BlockSpec((GROUP, features), lambda i, half: (half[0], 0)),
                pl.BlockSpec((1, features), lambda i, half: (0, 0)),
                pl.BlockSpec((1, features), lambda i, half: (0, 0)),
            ],
            out_specs=pl.BlockSpec((pieces, GROUP, PIECE), lambda i, half: (0, 0, 0)),
        ),
        compiler_params=pltpu.CompilerParams(vmem_limit_bytes=32 * 2**20),
        name="norm",
    )(half, hidden, gain, shift)


SMEM = pl.BlockSpec(memory_space=pltpu.SMEM)
VMEM = pl.BlockSpec(memory_space=pltpu.VMEM)
ORDER = (1, 3, 2)


def up_kernel(steps, at, ids, rows, weight, *rest):
    total = rest[-1]
    outs = rest[-1 - len(steps) : -1]
    h, x = at[0], at[1]
    for k, out in zip(steps, outs):
        target = lax.rem(x + k, NX)
        block_rows = rows[:, target].reshape(NY * GROUP, PIECE)
        total[...] = jnp.dot(block_rows, weight[...], preferred_element_type=F32)
        for y in range(NY):
            group = (y * NX + target) * (ROW // GROUP) + h
            for s in range(CAP):
                block = pl.multiple_of(ids[group, s] * BLOCK, BLOCK)
                picked = total[y * GROUP : (y + 1) * GROUP, pl.ds(block, BLOCK)]
                out[y, h, :, s * BLOCK : (s + 1) * BLOCK] = picked.astype(BF16)


def up(steps, at, ids, rows, weight, before=()):
    shape = jax.ShapeDtypeStruct((NY, ROW // GROUP, GROUP, CAP * BLOCK), BF16)
    return pl.pallas_call(
        functools.partial(up_kernel, steps),
        out_shape=[shape] * len(steps),
        in_specs=[SMEM, SMEM, VMEM, VMEM] + [VMEM] * len(before),
        out_specs=[VMEM] * len(steps),
        scratch_shapes=[pltpu.VMEM((NY * GROUP, weight.shape[1]), F32)],
        input_output_aliases={4 + i: i for i in range(len(before))},
        cost_estimate=pl.CostEstimate(
            flops=2 * len(steps) * NY * GROUP * weight.size, bytes_accessed=0, transcendentals=0
        ),
        compiler_params=pltpu.CompilerParams(vmem_limit_bytes=24 * 2**20),
        name="up_second" if before else "up_first",
    )(at, ids, rows, weight, *before)


def act_kernel(where, ids, valid, parts, bias, out):
    pre = jnp.sum(parts[...].astype(F32), axis=0)
    for g in range(ROW // GROUP):
        group = where[0] * (ROW // GROUP) + g
        for s in range(CAP):
            block = ids[group, s]
            keep = (s < valid[group]).astype(F32)
            mine = pre[g * GROUP : (g + 1) * GROUP, s * BLOCK : (s + 1) * BLOCK]
            value = (jnp.maximum(mine + bias[pl.ds(block, 1), :], 0.0) * keep).astype(BF16)
            for copy in range(out.shape[0]):
                out[copy, g * GROUP : (g + 1) * GROUP, s * BLOCK : (s + 1) * BLOCK] = value


def activate(where, ids, valid, parts, bias):
    return pl.pallas_call(
        act_kernel,
        out_shape=jax.ShapeDtypeStruct((NY, ROW, CAP * BLOCK), BF16),
        in_specs=[SMEM, SMEM, SMEM, VMEM, VMEM],
        out_specs=VMEM,
        compiler_params=pltpu.CompilerParams(vmem_limit_bytes=24 * 2**20),
        name="act",
    )(where, ids, valid, parts, bias)


def down_kernel(steps, where, ids, *rest):
    acts, weight = rest[: len(steps)], rest[len(steps)]
    keep, send, wide = rest[-3:]
    x, c = where[2], where[1]
    for k, ref in zip(steps, acts):
        source = lax.rem(x + NX - k, NX)
        wide[...] = jnp.zeros_like(wide)
        for y in range(NY):
            for g in range(ROW // GROUP):
                group = (y * NX + source) * (ROW // GROUP) + g
                low = y * ROW + g * GROUP
                for s in range(CAP):
                    at = pl.multiple_of(ids[group, s] * BLOCK, BLOCK)
                    wide[low : low + GROUP, pl.ds(at, BLOCK)] = ref[
                        y, g * GROUP : (g + 1) * GROUP, s * BLOCK : (s + 1) * BLOCK
                    ]
        value = jnp.dot(wide[...], weight[...], preferred_element_type=F32).astype(BF16)
        value = value.reshape(NY, ROW, PIECE)
        own, part = source // 2 == c, lax.rem(source, 2)

        @pl.when(own)
        def _():
            keep[:, part] = value

        @pl.when(jnp.logical_not(own))
        def _():
            send[:, part] = value


def down(steps, where, ids, acts, weight, before=()):
    return pl.pallas_call(
        functools.partial(down_kernel, steps),
        out_shape=[jax.ShapeDtypeStruct((NY, 2, ROW, PIECE), BF16)] * 2,
        in_specs=[SMEM, SMEM] + [VMEM] * (len(steps) + 1 + len(before)),
        out_specs=[VMEM, VMEM],
        scratch_shapes=[pltpu.VMEM((NY * ROW, weight.shape[0]), BF16)],
        input_output_aliases={3 + len(steps) + i: i for i in range(len(before))},
        cost_estimate=pl.CostEstimate(
            flops=2 * len(steps) * NY * ROW * weight.size, bytes_accessed=0, transcendentals=0
        ),
        compiler_params=pltpu.CompilerParams(vmem_limit_bytes=24 * 2**20),
        name="down",
    )(where, ids, *acts, weight, *before)


def body(
    hidden_in, norm_gain, norm_shift, up_weight, up_bias, down_weight, down_bias, active, counts
):
    y, x = lax.axis_index("y"), lax.axis_index("x")
    z, c = lax.axis_index("z"), lax.axis_index("c")
    r, t = y * NX + x, z * NC + c
    odd = lax.rem(r, 2) == 1
    ids, valid = active[:, 0, :], counts[:, 0]
    where = jnp.stack([r, c, x]).astype(jnp.int32)
    width = down_bias.shape[0]

    mine, others = jnp.stack([c, x]).astype(jnp.int32), jnp.stack([1 - c, x]).astype(jnp.int32)
    normed = norm(c.reshape(1), hidden_in, norm_gain.reshape(1, -1), norm_shift.reshape(1, -1))
    own = lax.all_to_all(normed, ("y", "x"), split_axis=0, concat_axis=0, tiled=True)
    other = lax.ppermute(own, "c", around(NC, 1))
    own, other = (v.reshape(NY, NX, GROUP, PIECE) for v in (own, other))
    first = up(ORDER + (0,), mine, ids, own, up_weight)
    sums = []
    for k, before in zip(ORDER + (0,), first):
        (part,) = up((k,), others, ids, other, up_weight, (before,))
        part = part.reshape(NY, ROW, CAP * BLOCK)
        sums.append(lax.ppermute(part, "x", around(NX, k)) if k else part)
    part = sum(v.astype(F32) for v in sums).astype(BF16)
    part = lax.all_to_all(part, "y", split_axis=0, concat_axis=0, tiled=True)
    bias = up_bias.astype(F32).reshape(-1, BLOCK)
    act = activate(where, ids, valid, part, bias)

    act = lax.all_to_all(act, "y", split_axis=0, concat_axis=0, tiled=True)
    keep, send = down((0,), where, ids, (act,), down_weight)
    for k in ORDER:
        moved = lax.ppermute(act, "x", around(NX, k))
        keep, send = down((k,), where, ids, (moved,), down_weight, (keep, send))
    got = lax.ppermute(send, "c", around(NC, 1))
    pair = (keep.astype(F32) + got.astype(F32)).astype(BF16).reshape(NZ, 2 * ROW, PIECE)
    pair = lax.all_to_all(pair, "z", split_axis=0, concat_axis=0, tiled=True)
    branch = jnp.sum(pair.astype(F32), axis=0).astype(BF16)

    back = [
        [
            (p * 16 + q, (2 * q + (j ^ (p & 1))) * 16 + p // 2)
            for p in range(32)
            for q in range(16)
        ]
        for j in range(2)
    ]
    low, high = branch[:ROW], branch[ROW:]
    first = lax.ppermute(jnp.where(odd, high, low), ALL, back[0])
    second = lax.ppermute(jnp.where(odd, low, high), ALL, back[1])
    summed = jnp.concatenate(
        [jnp.where(odd, second, first), jnp.where(odd, first, second)], axis=1
    ).astype(F32)
    resid = lax.dynamic_slice_in_dim(hidden_in, t * width, width, 1).astype(F32)
    return (resid + summed + down_bias.astype(F32)).astype(BF16)


def solution(mesh):
    fine = Mesh(mesh.devices.reshape(NY, NX, NZ, NC), ALL)
    dp, tensor = ("y", "x"), ("z", "c")
    placed = (
        P(dp, None),
        P(),
        P(),
        P(dp, tensor),
        P(tensor),
        P(tensor, dp),
        P(tensor),
        P(None, tensor, None),
        P(None, tensor),
    )
    return jax.shard_map(
        body, mesh=fine, in_specs=placed, out_specs=P(dp, tensor), check_vma=False
    )
```

```python
import functools
import itertools

import jax
import jax.numpy as jnp
from jax import lax
from jax.experimental import pallas as pl
from jax.experimental.pallas import tpu as pltpu
from jax.sharding import Mesh, PartitionSpec as P

BLOCK = 128
GROUP = 32
CAP = 4
NY, NX, NZ, NC = 8, 4, 8, 2
ROW = 64
PIECE = 384
F32 = jnp.float32
BF16 = jnp.bfloat16
ALL = ("y", "x", "z", "c")


def around(size, k):
    return [(i, (i + k) % size) for i in range(size)]


def norm_kernel(half, hidden, gain, shift, out):
    rows, features = hidden.shape
    pieces = features // PIECE
    gains = gain[...].astype(F32).reshape(1, features)
    shifts = shift[...].astype(F32).reshape(1, features)

    def piece(p):
        return hidden[:, p * PIECE : (p + 1) * PIECE].astype(F32)

    total = jnp.zeros((rows, PIECE), F32)
    for p in range(pieces):
        total += piece(p)
    mean = jnp.sum(total, axis=1, keepdims=True) / features
    total = jnp.zeros((rows, PIECE), F32)
    for p in range(pieces):
        center = piece(p) - mean
        total += center * center
    spread = jnp.sum(total, axis=1, keepdims=True) / features
    scale = lax.rsqrt(spread + 1e-05)
    for p in range(pieces):
        at = slice(p * PIECE, (p + 1) * PIECE)
        value = (piece(p) - mean) * scale * gains[:, at] + shifts[:, at]
        out[p] = value.astype(BF16)


def norm(half, hidden, gain, shift):
    features = hidden.shape[1]
    pieces = features // PIECE
    return pl.pallas_call(
        norm_kernel,
        out_shape=jax.ShapeDtypeStruct((pieces, GROUP, PIECE), BF16),
        grid_spec=pltpu.PrefetchScalarGridSpec(
            num_scalar_prefetch=1,
            grid=(1,),
            in_specs=[
                pl.BlockSpec((GROUP, features), lambda i, half: (half[0], 0)),
                pl.BlockSpec((features,), lambda i, half: (0,)),
                pl.BlockSpec((features,), lambda i, half: (0,)),
            ],
            out_specs=pl.BlockSpec((pieces, GROUP, PIECE), lambda i, half: (0, 0, 0)),
        ),
        compiler_params=pltpu.CompilerParams(vmem_limit_bytes=32 * 2**20),
        name="norm",
    )(half, hidden, gain, shift)


SMEM = pl.BlockSpec(memory_space=pltpu.SMEM)
VMEM = pl.BlockSpec(memory_space=pltpu.VMEM)
ORDER = (1, 3, 2)


def up_kernel(steps, at, ids, rows, weight, *rest):
    total = rest[-1]
    outs = rest[-1 - len(steps) : -1]
    h, x = at[0], at[1]
    for k, out in zip(steps, outs):
        target = lax.rem(x + k, NX)
        block_rows = rows[:, target].reshape(NY * GROUP, PIECE)
        total[...] = jnp.dot(block_rows, weight[...], preferred_element_type=F32)
        for y in range(NY):
            group = (y * NX + target) * (ROW // GROUP) + h
            for s in range(CAP):
                block = pl.multiple_of(ids[group, s] * BLOCK, BLOCK)
                picked = total[y * GROUP : (y + 1) * GROUP, pl.ds(block, BLOCK)]
                out[y, h, :, s * BLOCK : (s + 1) * BLOCK] = picked.astype(BF16)


def up(steps, at, ids, rows, weight, before=()):
    shape = jax.ShapeDtypeStruct((NY, ROW // GROUP, GROUP, CAP * BLOCK), BF16)
    return pl.pallas_call(
        functools.partial(up_kernel, steps),
        out_shape=[shape] * len(steps),
        in_specs=[SMEM, SMEM, VMEM, VMEM] + [VMEM] * len(before),
        out_specs=[VMEM] * len(steps),
        scratch_shapes=[pltpu.VMEM((NY * GROUP, weight.shape[1]), F32)],
        input_output_aliases={4 + i: i for i in range(len(before))},
        cost_estimate=pl.CostEstimate(
            flops=2 * len(steps) * NY * GROUP * weight.size, bytes_accessed=0, transcendentals=0
        ),
        compiler_params=pltpu.CompilerParams(vmem_limit_bytes=24 * 2**20),
        name="up_second" if before else "up_first",
    )(at, ids, rows, weight, *before)


def act_kernel(where, ids, valid, parts, bias, out):
    pre = jnp.sum(parts[...].astype(F32), axis=0)
    for g in range(ROW // GROUP):
        group = where[0] * (ROW // GROUP) + g
        for s in range(CAP):
            block = ids[group, s]
            keep = (s < valid[group]).astype(F32)
            mine = pre[g * GROUP : (g + 1) * GROUP, s * BLOCK : (s + 1) * BLOCK]
            value = (jnp.maximum(mine + bias[pl.ds(block, 1), :], 0.0) * keep).astype(BF16)
            for copy in range(out.shape[0]):
                out[copy, g * GROUP : (g + 1) * GROUP, s * BLOCK : (s + 1) * BLOCK] = value


def activate(where, ids, valid, parts, bias):
    return pl.pallas_call(
        act_kernel,
        out_shape=jax.ShapeDtypeStruct((NY, ROW, CAP * BLOCK), BF16),
        in_specs=[SMEM, SMEM, SMEM, VMEM, VMEM],
        out_specs=VMEM,
        compiler_params=pltpu.CompilerParams(vmem_limit_bytes=24 * 2**20),
        name="act",
    )(where, ids, valid, parts, bias)


TURNS = ((0, 0), (3, 1), (2, 3), (1, 2))


def down_kernel(turns, outs, where, ids, *rest):
    acts, weight = rest[: len(turns)], rest[len(turns)]
    (keep, *send), wide = rest[-1 - outs : -1], rest[-1]
    c, x, high = where[1], where[2], where[3]
    for turn, ref in zip(turns, acts):
        k = jnp.where(c == 0, TURNS[turn][0], TURNS[turn][1])
        source = lax.rem(x + NX - k, NX)
        wide[...] = jnp.zeros_like(wide)
        for y in range(NY):
            for g in range(ROW // GROUP):
                group = (y * NX + source) * (ROW // GROUP) + g
                low = y * ROW + g * GROUP
                for s in range(CAP):
                    at = pl.multiple_of(ids[group, s] * BLOCK, BLOCK)
                    wide[low : low + GROUP, pl.ds(at, BLOCK)] = ref[
                        y, g * GROUP : (g + 1) * GROUP, s * BLOCK : (s + 1) * BLOCK
                    ]
        value = jnp.dot(wide[...], weight[...], preferred_element_type=F32).astype(BF16)
        value = value.reshape(NY, ROW, PIECE)
        part = lax.rem(k, 2)

        def put(ref, value=value, part=part):
            for y in range(NY):
                ref[lax.rem(y + NZ - high, NZ), part] = value[y]

        own = [k_of // 2 == core for core, k_of in enumerate(TURNS[turn])]
        if own[0] == own[1]:
            put(keep if own[0] else send[0])
        else:
            pl.when(c == own.index(True))(functools.partial(put, keep))
            pl.when(c == own.index(False))(functools.partial(put, send[0]))


def down(turns, where, ids, acts, weight, before=()):
    outs = len(before) or 2
    return pl.pallas_call(
        functools.partial(down_kernel, turns, outs),
        out_shape=[jax.ShapeDtypeStruct((NY, 2, ROW, PIECE), BF16)] * outs,
        in_specs=[SMEM, SMEM] + [VMEM] * (len(turns) + 1 + len(before)),
        out_specs=[VMEM] * outs,
        scratch_shapes=[pltpu.VMEM((NY * ROW, weight.shape[0]), BF16)],
        input_output_aliases={3 + len(turns) + i: i for i in range(len(before))},
        cost_estimate=pl.CostEstimate(
            flops=(32 if outs == 1 else 1) * 2 * len(turns) * NY * ROW * weight.size,
            bytes_accessed=0,
            transcendentals=0,
        ),
        compiler_params=pltpu.CompilerParams(vmem_limit_bytes=24 * 2**20),
        name="down",
    )(where, ids, *acts, weight, *before)


def turn_pairs(turn):
    return [
        (x * NC + c, (x + TURNS[turn][c]) % NX * NC + c) for x in range(NX) for c in range(NC)
    ]


def body(
    hidden_in, norm_gain, norm_shift, up_weight, up_bias, down_weight, down_bias, active, counts
):
    y, x = lax.axis_index("y"), lax.axis_index("x")
    z, c = lax.axis_index("z"), lax.axis_index("c")
    r, t = y * NX + x, z * NC + c
    odd = lax.rem(r, 2) == 1
    ids, valid = active[:, 0, :], counts[:, 0]
    where = jnp.stack([r, c, x, y]).astype(jnp.int32)
    width = down_bias.shape[0]

    mine, others = jnp.stack([c, x]).astype(jnp.int32), jnp.stack([1 - c, x]).astype(jnp.int32)
    normed = norm(c.reshape(1), hidden_in, norm_gain, norm_shift)
    own = lax.all_to_all(normed, ("y", "x"), split_axis=0, concat_axis=0, tiled=True)
    other = lax.ppermute(own, "c", around(NC, 1))
    own, other = (v.reshape(NY, NX, GROUP, PIECE) for v in (own, other))
    first = up(ORDER + (0,), mine, ids, own, up_weight)
    sums = []
    for k, before in zip(ORDER + (0,), first):
        (part,) = up((k,), others, ids, other, up_weight, (before,))
        part = part.reshape(NY, ROW, CAP * BLOCK)
        sums.append(lax.ppermute(part, "x", around(NX, k)) if k else part)
    part = sum(v.astype(F32) for v in sums).astype(BF16)
    part = lax.all_to_all(part, "y", split_axis=0, concat_axis=0, tiled=True)
    bias = up_bias.astype(F32).reshape(-1, BLOCK)
    act = activate(where, ids, valid, part, bias)

    act = lax.all_to_all(act, "y", split_axis=0, concat_axis=0, tiled=True)
    keep, send = down((0,), where, ids, (act,), down_weight)
    for turn in (1, 2):
        moved = lax.ppermute(act, ("x", "c"), turn_pairs(turn))
        keep, send = down((turn,), where, ids, (moved,), down_weight, (keep, send))
    got = lax.ppermute(send, "c", around(NC, 1))
    moved = lax.ppermute(act, ("x", "c"), turn_pairs(3))
    (keep,) = down((3,), where, ids, (moved,), down_weight, (keep,))
    pair = (keep.astype(F32) + got.astype(F32)).astype(BF16).reshape(NZ, 2 * ROW, PIECE)
    pair = lax.all_to_all(pair, "z", split_axis=0, concat_axis=0, tiled=True)
    branch = jnp.sum(pair.astype(F32), axis=0).astype(BF16)

    back = [[], []]
    for j, ys, xs, zs, cs in itertools.product(range(2), *map(range, (NY, NX, NZ, NC))):
        row = (zs + ys) % NY * NX + (xs - 2 * cs - j) % NX
        source = ((ys * NX + xs) * NZ + zs) * NC + cs
        back[j].append((source, row * NZ * NC + (ys * NX + xs) // 2))
    first = lax.ppermute(branch[:ROW], ALL, back[0])
    second = lax.ppermute(branch[ROW:], ALL, back[1])
    summed = jnp.concatenate(
        [jnp.where(odd, second, first), jnp.where(odd, first, second)], axis=1
    ).astype(F32)
    resid = lax.dynamic_slice_in_dim(hidden_in, t * width, width, 1).astype(F32)
    return (resid + summed + down_bias.astype(F32)).astype(BF16)


def solution(mesh):
    fine = Mesh(mesh.devices.reshape(NY, NX, NZ, NC), ALL)
    dp, tensor = ("y", "x"), ("z", "c")
    placed = (
        P(dp, None),
        P(),
        P(),
        P(dp, tensor),
        P(tensor),
        P(tensor, dp),
        P(tensor),
        P(None, tensor, None),
        P(None, tensor),
    )
    return jax.shard_map(
        body, mesh=fine, in_specs=placed, out_specs=P(dp, tensor), check_vma=False
    )
```

```python
import functools
import itertools

import jax
import jax.numpy as jnp
from jax import lax
from jax.experimental import pallas as pl
from jax.experimental.pallas import tpu as pltpu
from jax.sharding import Mesh, PartitionSpec as P

BLOCK = 128
GROUP = 32
CAP = 4
NY, NX, NZ, NC = 8, 4, 8, 2
ROW = 64
PIECE = 384
F32 = jnp.float32
BF16 = jnp.bfloat16
ALL = ("y", "x", "z", "c")


def around(size, k):
    return [(i, (i + k) % size) for i in range(size)]


def norm_kernel(half, hidden, scales, out):
    rows, features = hidden.shape
    pieces = features // PIECE

    def piece(p):
        return hidden[:, p * PIECE : (p + 1) * PIECE].astype(F32)

    total = jnp.zeros((rows, PIECE), F32)
    for p in range(pieces):
        total += piece(p)
    mean = jnp.sum(total, axis=1, keepdims=True) / features
    total = jnp.zeros((rows, PIECE), F32)
    for p in range(pieces):
        center = piece(p) - mean
        total += center * center
    spread = jnp.sum(total, axis=1, keepdims=True) / features
    scale = lax.rsqrt(spread + 1e-05)
    for p in range(pieces):
        at = slice(p * PIECE, (p + 1) * PIECE)
        value = (piece(p) - mean) * scale * scales[0:1, at] + scales[1:2, at]
        out[p] = value.astype(BF16)


def norm(half, hidden, scales):
    features = hidden.shape[1]
    pieces = features // PIECE
    return pl.pallas_call(
        norm_kernel,
        out_shape=jax.ShapeDtypeStruct((pieces, GROUP, PIECE), BF16),
        grid_spec=pltpu.PrefetchScalarGridSpec(
            num_scalar_prefetch=1,
            grid=(1,),
            in_specs=[
                pl.BlockSpec((GROUP, features), lambda i, half: (half[0], 0)),
                pl.BlockSpec((2, features), lambda i, half: (0, 0)),
            ],
            out_specs=pl.BlockSpec((pieces, GROUP, PIECE), lambda i, half: (0, 0, 0)),
        ),
        compiler_params=pltpu.CompilerParams(vmem_limit_bytes=32 * 2**20),
        name="norm",
    )(half, hidden, scales)


SMEM = pl.BlockSpec(memory_space=pltpu.SMEM)
VMEM = pl.BlockSpec(memory_space=pltpu.VMEM)
LEAVES = ((1, 3), (3, 1), (2, 2), (0, 0))


def up_kernel(turns, at, ids, rows, weight, *rest):
    total = rest[-1]
    outs = rest[-1 - len(turns) : -1]
    h, x, c = at[0], at[1], at[2]
    for turn, out in zip(turns, outs):
        k = jnp.where(c == 0, LEAVES[turn][0], LEAVES[turn][1])
        target = lax.rem(x + k, NX)
        block_rows = rows[:, target].reshape(NY * GROUP, PIECE)
        total[...] = jnp.dot(block_rows, weight[...], preferred_element_type=F32)
        for y in range(NY):
            group = (y * NX + target) * (ROW // GROUP) + h
            for s in range(CAP):
                block = pl.multiple_of(ids[group, s] * BLOCK, BLOCK)
                picked = total[y * GROUP : (y + 1) * GROUP, pl.ds(block, BLOCK)]
                out[y, h, :, s * BLOCK : (s + 1) * BLOCK] = picked.astype(BF16)


def up(turns, at, ids, rows, weight, before=()):
    shape = jax.ShapeDtypeStruct((NY, ROW // GROUP, GROUP, CAP * BLOCK), BF16)
    return pl.pallas_call(
        functools.partial(up_kernel, turns),
        out_shape=[shape] * len(turns),
        in_specs=[SMEM, SMEM, VMEM, VMEM] + [VMEM] * len(before),
        out_specs=[VMEM] * len(turns),
        scratch_shapes=[pltpu.VMEM((NY * GROUP, weight.shape[1]), F32)],
        input_output_aliases={4 + i: i for i in range(len(before))},
        cost_estimate=pl.CostEstimate(
            flops=2 * len(turns) * NY * GROUP * weight.size,
            bytes_accessed=0,
            transcendentals=0,
        ),
        compiler_params=pltpu.CompilerParams(vmem_limit_bytes=24 * 2**20),
        name="up_second" if before else "up_first",
    )(at, ids, rows, weight, *before)


def act_kernel(where, ids, valid, parts, bias, out):
    pre = jnp.sum(parts[...].astype(F32), axis=0)
    for g in range(ROW // GROUP):
        group = where[0] * (ROW // GROUP) + g
        for s in range(CAP):
            block = ids[group, s]
            keep = (s < valid[group]).astype(F32)
            mine = pre[g * GROUP : (g + 1) * GROUP, s * BLOCK : (s + 1) * BLOCK]
            value = (jnp.maximum(mine + bias[pl.ds(block, 1), :], 0.0) * keep).astype(BF16)
            for copy in range(out.shape[0]):
                out[copy, g * GROUP : (g + 1) * GROUP, s * BLOCK : (s + 1) * BLOCK] = value


def activate(where, ids, valid, parts, bias):
    return pl.pallas_call(
        act_kernel,
        out_shape=jax.ShapeDtypeStruct((NY, ROW, CAP * BLOCK), BF16),
        in_specs=[SMEM, SMEM, SMEM, VMEM, VMEM],
        out_specs=VMEM,
        compiler_params=pltpu.CompilerParams(vmem_limit_bytes=24 * 2**20),
        name="act",
    )(where, ids, valid, parts, bias)


TURNS = ((0, 0), (3, 1), (2, 3), (1, 2))


def down_kernel(turns, outs, where, ids, *rest):
    acts, weight = rest[: len(turns)], rest[len(turns)]
    (keep, *send), wide = rest[-1 - outs : -1], rest[-1]
    c, x, high = where[1], where[2], where[3]
    for turn, ref in zip(turns, acts):
        k = jnp.where(c == 0, TURNS[turn][0], TURNS[turn][1])
        source = lax.rem(x + NX - k, NX)
        wide[...] = jnp.zeros_like(wide)
        for y in range(NY):
            for g in range(ROW // GROUP):
                group = (y * NX + source) * (ROW // GROUP) + g
                low = y * ROW + g * GROUP
                for s in range(CAP):
                    at = pl.multiple_of(ids[group, s] * BLOCK, BLOCK)
                    wide[low : low + GROUP, pl.ds(at, BLOCK)] = ref[
                        y, g * GROUP : (g + 1) * GROUP, s * BLOCK : (s + 1) * BLOCK
                    ]
        value = jnp.dot(wide[...], weight[...], preferred_element_type=F32).astype(BF16)
        value = value.reshape(NY, ROW, PIECE)
        part = lax.rem(k, 2)

        def put(ref, value=value, part=part):
            for y in range(NY):
                ref[lax.rem(y + NZ - high, NZ), part] = value[y]

        own = [k_of // 2 == core for core, k_of in enumerate(TURNS[turn])]
        if own[0] == own[1]:
            put(keep if own[0] else send[0])
        else:
            pl.when(c == own.index(True))(functools.partial(put, keep))
            pl.when(c == own.index(False))(functools.partial(put, send[0]))


def down(turns, where, ids, acts, weight, before=()):
    outs = len(before) or 2
    return pl.pallas_call(
        functools.partial(down_kernel, turns, outs),
        out_shape=[jax.ShapeDtypeStruct((NY, 2, ROW, PIECE), BF16)] * outs,
        in_specs=[SMEM, SMEM] + [VMEM] * (len(turns) + 1 + len(before)),
        out_specs=[VMEM] * outs,
        scratch_shapes=[pltpu.VMEM((NY * ROW, weight.shape[0]), BF16)],
        input_output_aliases={3 + len(turns) + i: i for i in range(len(before))},
        cost_estimate=pl.CostEstimate(
            flops=(32 if outs == 1 else 1) * 2 * len(turns) * NY * ROW * weight.size,
            bytes_accessed=0,
            transcendentals=0,
        ),
        compiler_params=pltpu.CompilerParams(vmem_limit_bytes=24 * 2**20),
        name="down",
    )(where, ids, *acts, weight, *before)


def pairs(steps):
    return [(x * NC + c, (x + steps[c]) % NX * NC + c) for x in range(NX) for c in range(NC)]


def body(
    hidden_in, norm_gain, norm_shift, up_weight, up_bias, down_weight, down_bias, active, counts
):
    y, x = lax.axis_index("y"), lax.axis_index("x")
    z, c = lax.axis_index("z"), lax.axis_index("c")
    r, t = y * NX + x, z * NC + c
    odd = lax.rem(r, 2) == 1
    ids, valid = active[:, 0, :], counts[:, 0]
    where = jnp.stack([r, c, x, y]).astype(jnp.int32)
    width = down_bias.shape[0]

    mine = jnp.stack([c, x, c]).astype(jnp.int32)
    others = jnp.stack([1 - c, x, c]).astype(jnp.int32)
    scales = jnp.stack([norm_gain, norm_shift]).astype(F32)
    normed = norm(c.reshape(1), hidden_in, scales)
    own = lax.all_to_all(normed, ("y", "x"), split_axis=0, concat_axis=0, tiled=True)
    other = lax.ppermute(own, "c", around(NC, 1))
    own, other = (v.reshape(NY, NX, GROUP, PIECE) for v in (own, other))
    first = up((0, 1, 2, 3), mine, ids, own, up_weight)
    parts = []
    for turn, before in enumerate(first):
        (part,) = up((turn,), others, ids, other, up_weight, (before,))
        part = part.reshape(NY, ROW, CAP * BLOCK)
        leaves = LEAVES[turn]
        parts.append(lax.ppermute(part, ("x", "c"), pairs(leaves)) if any(leaves) else part)
    part = sum(v.astype(F32) for v in parts).astype(BF16)
    part = lax.all_to_all(part, "y", split_axis=0, concat_axis=0, tiled=True)
    bias = up_bias.astype(F32).reshape(-1, BLOCK)
    act = activate(where, ids, valid, part, bias)

    act = lax.all_to_all(act, "y", split_axis=0, concat_axis=0, tiled=True)
    keep, send = down((0,), where, ids, (act,), down_weight)
    for turn in (1, 2):
        moved = lax.ppermute(act, ("x", "c"), pairs(TURNS[turn]))
        keep, send = down((turn,), where, ids, (moved,), down_weight, (keep, send))
    got = lax.ppermute(send, "c", around(NC, 1))
    moved = lax.ppermute(act, ("x", "c"), pairs(TURNS[3]))
    (keep,) = down((3,), where, ids, (moved,), down_weight, (keep,))
    pair = (keep.astype(F32) + got.astype(F32)).astype(BF16).reshape(NZ, 2 * ROW, PIECE)
    pair = lax.all_to_all(pair, "z", split_axis=0, concat_axis=0, tiled=True)
    branch = jnp.sum(pair.astype(F32), axis=0).astype(BF16)

    back = [[], []]
    for j, ys, xs, zs, cs in itertools.product(range(2), *map(range, (NY, NX, NZ, NC))):
        row = (zs + ys) % NY * NX + (xs - 2 * cs - j) % NX
        source = ((ys * NX + xs) * NZ + zs) * NC + cs
        back[j].append((source, row * NZ * NC + (ys * NX + xs) // 2))
    first = lax.ppermute(branch[:ROW], ALL, back[0])
    second = lax.ppermute(branch[ROW:], ALL, back[1])
    summed = jnp.concatenate(
        [jnp.where(odd, second, first), jnp.where(odd, first, second)], axis=1
    ).astype(F32)
    resid = lax.dynamic_slice_in_dim(hidden_in, t * width, width, 1).astype(F32)
    return (resid + summed + down_bias.astype(F32)).astype(BF16)


def solution(mesh):
    fine = Mesh(mesh.devices.reshape(NY, NX, NZ, NC), ALL)
    dp, tensor = ("y", "x"), ("z", "c")
    placed = (
        P(dp, None),
        P(),
        P(),
        P(dp, tensor),
        P(tensor),
        P(tensor, dp),
        P(tensor),
        P(None, tensor, None),
        P(None, tensor),
    )
    return jax.shard_map(
        body, mesh=fine, in_specs=placed, out_specs=P(dp, tensor), check_vma=False
    )
```

```python
import functools
import itertools

import jax
import jax.numpy as jnp
from jax import lax
from jax.experimental import pallas as pl
from jax.experimental.pallas import tpu as pltpu
from jax.sharding import Mesh, PartitionSpec as P

BLOCK = 128
GROUP = 32
CAP = 4
NY, NX, NZ, NC = 8, 4, 8, 2
ROW = 64
PIECE = 384
F32 = jnp.float32
BF16 = jnp.bfloat16
ALL = ("y", "x", "z", "c")


def around(size, k):
    return [(i, (i + k) % size) for i in range(size)]


def norm_kernel(half, hidden, scales, out):
    rows, features = hidden.shape
    pieces = features // PIECE

    def piece(p):
        return hidden[:, p * PIECE : (p + 1) * PIECE].astype(F32)

    total = jnp.zeros((rows, PIECE), F32)
    for p in range(pieces):
        total += piece(p)
    mean = jnp.sum(total, axis=1, keepdims=True) / features
    total = jnp.zeros((rows, PIECE), F32)
    for p in range(pieces):
        center = piece(p) - mean
        total += center * center
    spread = jnp.sum(total, axis=1, keepdims=True) / features
    scale = lax.rsqrt(spread + 1e-05)
    for p in range(pieces):
        at = slice(p * PIECE, (p + 1) * PIECE)
        value = (piece(p) - mean) * scale * scales[0:1, at] + scales[1:2, at]
        out[p] = value.astype(BF16)


def norm(half, hidden, scales):
    features = hidden.shape[1]
    pieces = features // PIECE
    return pl.pallas_call(
        norm_kernel,
        out_shape=jax.ShapeDtypeStruct((pieces, GROUP, PIECE), BF16),
        grid_spec=pltpu.PrefetchScalarGridSpec(
            num_scalar_prefetch=1,
            grid=(1,),
            in_specs=[
                pl.BlockSpec((GROUP, features), lambda i, half: (half[0], 0)),
                pl.BlockSpec((2, features), lambda i, half: (0, 0)),
            ],
            out_specs=pl.BlockSpec((pieces, GROUP, PIECE), lambda i, half: (0, 0, 0)),
        ),
        compiler_params=pltpu.CompilerParams(vmem_limit_bytes=32 * 2**20),
        name="norm",
    )(half, hidden, scales)


SMEM = pl.BlockSpec(memory_space=pltpu.SMEM)
VMEM = pl.BlockSpec(memory_space=pltpu.VMEM)
LEAVES = ((2, 2), (3, 1), (1, 3), (0, 0))


def up_kernel(turns, at, ids, rows, weight, *rest):
    total = rest[-1]
    outs = rest[-1 - len(turns) : -1]
    h, x, c = at[0], at[1], at[2]
    for turn, out in zip(turns, outs):
        k = jnp.where(c == 0, LEAVES[turn][0], LEAVES[turn][1])
        target = lax.rem(x + k, NX)
        block_rows = rows[:, target].reshape(NY * GROUP, PIECE)
        total[...] = jnp.dot(block_rows, weight[...], preferred_element_type=F32)
        for y in range(NY):
            group = (y * NX + target) * (ROW // GROUP) + h
            for s in range(CAP):
                block = pl.multiple_of(ids[group, s] * BLOCK, BLOCK)
                picked = total[y * GROUP : (y + 1) * GROUP, pl.ds(block, BLOCK)]
                out[y, h, :, s * BLOCK : (s + 1) * BLOCK] = picked.astype(BF16)


def up(turns, at, ids, rows, weight, before=()):
    shape = jax.ShapeDtypeStruct((NY, ROW // GROUP, GROUP, CAP * BLOCK), BF16)
    return pl.pallas_call(
        functools.partial(up_kernel, turns),
        out_shape=[shape] * len(turns),
        in_specs=[SMEM, SMEM, VMEM, VMEM] + [VMEM] * len(before),
        out_specs=[VMEM] * len(turns),
        scratch_shapes=[pltpu.VMEM((NY * GROUP, weight.shape[1]), F32)],
        input_output_aliases={4 + i: i for i in range(len(before))},
        cost_estimate=pl.CostEstimate(
            flops=2 * len(turns) * NY * GROUP * weight.size,
            bytes_accessed=0,
            transcendentals=0,
        ),
        compiler_params=pltpu.CompilerParams(vmem_limit_bytes=24 * 2**20),
        name="up_second" if before else "up_first",
    )(at, ids, rows, weight, *before)


def act_kernel(where, ids, valid, parts, bias, out):
    pre = jnp.sum(parts[...].astype(F32), axis=0)
    for g in range(ROW // GROUP):
        group = where[0] * (ROW // GROUP) + g
        for s in range(CAP):
            block = ids[group, s]
            keep = (s < valid[group]).astype(F32)
            mine = pre[g * GROUP : (g + 1) * GROUP, s * BLOCK : (s + 1) * BLOCK]
            value = (jnp.maximum(mine + bias[pl.ds(block, 1), :], 0.0) * keep).astype(BF16)
            for copy in range(out.shape[0]):
                out[copy, g * GROUP : (g + 1) * GROUP, s * BLOCK : (s + 1) * BLOCK] = value


def activate(where, ids, valid, parts, bias):
    return pl.pallas_call(
        act_kernel,
        out_shape=jax.ShapeDtypeStruct((NY, ROW, CAP * BLOCK), BF16),
        in_specs=[SMEM, SMEM, SMEM, VMEM, VMEM],
        out_specs=VMEM,
        compiler_params=pltpu.CompilerParams(vmem_limit_bytes=24 * 2**20),
        name="act",
    )(where, ids, valid, parts, bias)


TURNS = ((0, 0), (3, 1), (2, 3), (1, 2))


def down_kernel(turns, outs, where, ids, *rest):
    acts, weight = rest[: len(turns)], rest[len(turns)]
    (keep, *send), wide = rest[-1 - outs : -1], rest[-1]
    c, x, high = where[1], where[2], where[3]
    for turn, ref in zip(turns, acts):
        k = jnp.where(c == 0, TURNS[turn][0], TURNS[turn][1])
        source = lax.rem(x + NX - k, NX)
        wide[...] = jnp.zeros_like(wide)
        for y in range(NY):
            for g in range(ROW // GROUP):
                group = (y * NX + source) * (ROW // GROUP) + g
                low = y * ROW + g * GROUP
                for s in range(CAP):
                    at = pl.multiple_of(ids[group, s] * BLOCK, BLOCK)
                    wide[low : low + GROUP, pl.ds(at, BLOCK)] = ref[
                        y, g * GROUP : (g + 1) * GROUP, s * BLOCK : (s + 1) * BLOCK
                    ]
        value = jnp.dot(wide[...], weight[...], preferred_element_type=F32).astype(BF16)
        value = value.reshape(NY, ROW, PIECE)
        part = lax.rem(k, 2)

        def put(ref, value=value, part=part):
            for y in range(NY):
                ref[lax.rem(y + NZ - high, NZ), part] = value[y]

        own = [k_of // 2 == core for core, k_of in enumerate(TURNS[turn])]
        if own[0] == own[1]:
            put(keep if own[0] else send[0])
        else:
            pl.when(c == own.index(True))(functools.partial(put, keep))
            pl.when(c == own.index(False))(functools.partial(put, send[0]))


def down(turns, where, ids, acts, weight, before=()):
    outs = len(before) or 2
    return pl.pallas_call(
        functools.partial(down_kernel, turns, outs),
        out_shape=[jax.ShapeDtypeStruct((NY, 2, ROW, PIECE), BF16)] * outs,
        in_specs=[SMEM, SMEM] + [VMEM] * (len(turns) + 1 + len(before)),
        out_specs=[VMEM] * outs,
        scratch_shapes=[pltpu.VMEM((NY * ROW, weight.shape[0]), BF16)],
        input_output_aliases={3 + len(turns) + i: i for i in range(len(before))},
        cost_estimate=pl.CostEstimate(
            flops=(32 if outs == 1 else 1) * 2 * len(turns) * NY * ROW * weight.size,
            bytes_accessed=0,
            transcendentals=0,
        ),
        compiler_params=pltpu.CompilerParams(vmem_limit_bytes=24 * 2**20),
        name="down",
    )(where, ids, *acts, weight, *before)


def pairs(steps):
    return [(x * NC + c, (x + steps[c]) % NX * NC + c) for x in range(NX) for c in range(NC)]


def body(
    hidden_in, norm_gain, norm_shift, up_weight, up_bias, down_weight, down_bias, active, counts
):
    y, x = lax.axis_index("y"), lax.axis_index("x")
    z, c = lax.axis_index("z"), lax.axis_index("c")
    r, t = y * NX + x, z * NC + c
    odd = lax.rem(r, 2) == 1
    ids, valid = active[:, 0, :], counts[:, 0]
    where = jnp.stack([r, c, x, y]).astype(jnp.int32)
    width = down_bias.shape[0]

    mine = jnp.stack([c, x, c]).astype(jnp.int32)
    others = jnp.stack([1 - c, x, c]).astype(jnp.int32)
    scales = jnp.stack([norm_gain, norm_shift]).astype(F32)
    normed = norm(c.reshape(1), hidden_in, scales)
    own = lax.all_to_all(normed, ("y", "x"), split_axis=0, concat_axis=0, tiled=True)
    other = lax.ppermute(own, "c", around(NC, 1))
    own, other = (v.reshape(NY, NX, GROUP, PIECE) for v in (own, other))
    first = up((0, 1, 2, 3), mine, ids, own, up_weight)
    parts = []
    for turn, before in enumerate(first):
        (part,) = up((turn,), others, ids, other, up_weight, (before,))
        parts.append(part.reshape(NY, ROW, CAP * BLOCK))
    passed = lax.ppermute(parts[0], ("x", "c"), pairs(LEAVES[2]))
    direct = lax.ppermute(parts[1], ("x", "c"), pairs(LEAVES[1]))
    joined = (parts[2].astype(F32) + passed.astype(F32)).astype(BF16)
    joined = lax.ppermute(joined, ("x", "c"), pairs(LEAVES[2]))
    part = (parts[3].astype(F32) + direct.astype(F32) + joined.astype(F32)).astype(BF16)
    part = lax.all_to_all(part, "y", split_axis=0, concat_axis=0, tiled=True)
    bias = up_bias.astype(F32).reshape(-1, BLOCK)
    act = activate(where, ids, valid, part, bias)

    act = lax.all_to_all(act, "y", split_axis=0, concat_axis=0, tiled=True)
    keep, send = down((0,), where, ids, (act,), down_weight)
    for turn in (1, 2):
        moved = lax.ppermute(act, ("x", "c"), pairs(TURNS[turn]))
        keep, send = down((turn,), where, ids, (moved,), down_weight, (keep, send))
    got = lax.ppermute(send, "c", around(NC, 1))
    moved = lax.ppermute(act, ("x", "c"), pairs(TURNS[3]))
    (keep,) = down((3,), where, ids, (moved,), down_weight, (keep,))
    pair = (keep.astype(F32) + got.astype(F32)).astype(BF16).reshape(NZ, 2 * ROW, PIECE)
    pair = lax.all_to_all(pair, "z", split_axis=0, concat_axis=0, tiled=True)
    branch = jnp.sum(pair.astype(F32), axis=0).astype(BF16)

    back = [[], []]
    for j, ys, xs, zs, cs in itertools.product(range(2), *map(range, (NY, NX, NZ, NC))):
        row = (zs + ys) % NY * NX + (xs - 2 * cs - j) % NX
        source = ((ys * NX + xs) * NZ + zs) * NC + cs
        back[j].append((source, row * NZ * NC + (ys * NX + xs) // 2))
    first = lax.ppermute(branch[:ROW], ALL, back[0])
    second = lax.ppermute(branch[ROW:], ALL, back[1])
    summed = jnp.concatenate(
        [jnp.where(odd, second, first), jnp.where(odd, first, second)], axis=1
    ).astype(F32)
    resid = lax.dynamic_slice_in_dim(hidden_in, t * width, width, 1).astype(F32)
    return (resid + summed + down_bias.astype(F32)).astype(BF16)


def solution(mesh):
    fine = Mesh(mesh.devices.reshape(NY, NX, NZ, NC), ALL)
    dp, tensor = ("y", "x"), ("z", "c")
    placed = (
        P(dp, None),
        P(),
        P(),
        P(dp, tensor),
        P(tensor),
        P(tensor, dp),
        P(tensor),
        P(None, tensor, None),
        P(None, tensor),
    )
    return jax.shard_map(
        body, mesh=fine, in_specs=placed, out_specs=P(dp, tensor), check_vma=False
    )
```

```python
import functools
import itertools

import jax
import jax.numpy as jnp
from jax import lax
from jax.experimental import pallas as pl
from jax.experimental.pallas import tpu as pltpu
from jax.sharding import Mesh, PartitionSpec as P

BLOCK = 128
GROUP = 32
CAP = 4
NY, NX, NZ, NC = 8, 4, 8, 2
ROW = 64
PIECE = 384
F32 = jnp.float32
BF16 = jnp.bfloat16
ALL = ("y", "x", "z", "c")


def around(size, k):
    return [(i, (i + k) % size) for i in range(size)]


def norm_kernel(half, hidden, scales, out):
    rows, features = hidden.shape
    pieces = features // PIECE

    def piece(p):
        return hidden[:, p * PIECE : (p + 1) * PIECE].astype(F32)

    total = jnp.zeros((rows, PIECE), F32)
    for p in range(pieces):
        total += piece(p)
    mean = jnp.sum(total, axis=1, keepdims=True) / features
    total = jnp.zeros((rows, PIECE), F32)
    for p in range(pieces):
        center = piece(p) - mean
        total += center * center
    spread = jnp.sum(total, axis=1, keepdims=True) / features
    scale = lax.rsqrt(spread + 1e-05)
    for p in range(pieces):
        at = slice(p * PIECE, (p + 1) * PIECE)
        value = (piece(p) - mean) * scale * scales[0:1, at] + scales[1:2, at]
        out[p] = value.astype(BF16)


def norm(half, hidden, scales):
    features = hidden.shape[1]
    pieces = features // PIECE
    return pl.pallas_call(
        norm_kernel,
        out_shape=jax.ShapeDtypeStruct((pieces, GROUP, PIECE), BF16),
        grid_spec=pltpu.PrefetchScalarGridSpec(
            num_scalar_prefetch=1,
            grid=(1,),
            in_specs=[
                pl.BlockSpec((GROUP, features), lambda i, half: (half[0], 0)),
                pl.BlockSpec((2, features), lambda i, half: (0, 0)),
            ],
            out_specs=pl.BlockSpec((pieces, GROUP, PIECE), lambda i, half: (0, 0, 0)),
        ),
        compiler_params=pltpu.CompilerParams(vmem_limit_bytes=32 * 2**20),
        name="norm",
    )(half, hidden, scales)


SMEM = pl.BlockSpec(memory_space=pltpu.SMEM)
VMEM = pl.BlockSpec(memory_space=pltpu.VMEM)
LEAVES = ((2, 2), (3, 1), (1, 3), (0, 0))


def up_kernel(turns, at, ids, rows, weight, *rest):
    total = rest[-1]
    outs = rest[-1 - len(turns) : -1]
    h, x, c = at[0], at[1], at[2]
    for turn, out in zip(turns, outs):
        k = jnp.where(c == 0, LEAVES[turn][0], LEAVES[turn][1])
        target = lax.rem(x + k, NX)
        block_rows = rows[:, target].reshape(NY * GROUP, PIECE)
        total[...] = jnp.dot(block_rows, weight[...], preferred_element_type=F32)
        for y in range(NY):
            group = (y * NX + target) * (ROW // GROUP) + h
            for s in range(CAP):
                block = pl.multiple_of(ids[group, s] * BLOCK, BLOCK)
                picked = total[y * GROUP : (y + 1) * GROUP, pl.ds(block, BLOCK)]
                out[y, h, :, s * BLOCK : (s + 1) * BLOCK] = picked.astype(BF16)


def up(turns, at, ids, rows, weight, before=()):
    shape = jax.ShapeDtypeStruct((NY, ROW // GROUP, GROUP, CAP * BLOCK), BF16)
    return pl.pallas_call(
        functools.partial(up_kernel, turns),
        out_shape=[shape] * len(turns),
        in_specs=[SMEM, SMEM, VMEM, VMEM] + [VMEM] * len(before),
        out_specs=[VMEM] * len(turns),
        scratch_shapes=[pltpu.VMEM((NY * GROUP, weight.shape[1]), F32)],
        input_output_aliases={4 + i: i for i in range(len(before))},
        cost_estimate=pl.CostEstimate(
            flops=2 * len(turns) * NY * GROUP * weight.size,
            bytes_accessed=0,
            transcendentals=0,
        ),
        compiler_params=pltpu.CompilerParams(vmem_limit_bytes=24 * 2**20),
        name="up_second" if before else "up_first",
    )(at, ids, rows, weight, *before)


def act_kernel(where, ids, valid, parts, bias, out):
    pre = jnp.sum(parts[...].astype(F32), axis=0)
    for g in range(ROW // GROUP):
        group = where[0] * (ROW // GROUP) + g
        for s in range(CAP):
            block = ids[group, s]
            keep = (s < valid[group]).astype(F32)
            mine = pre[g * GROUP : (g + 1) * GROUP, s * BLOCK : (s + 1) * BLOCK]
            value = (jnp.maximum(mine + bias[pl.ds(block, 1), :], 0.0) * keep).astype(BF16)
            for copy in range(out.shape[0]):
                out[copy, g * GROUP : (g + 1) * GROUP, s * BLOCK : (s + 1) * BLOCK] = value


def activate(where, ids, valid, parts, bias):
    return pl.pallas_call(
        act_kernel,
        out_shape=jax.ShapeDtypeStruct((NY, ROW, CAP * BLOCK), BF16),
        in_specs=[SMEM, SMEM, SMEM, VMEM, VMEM],
        out_specs=VMEM,
        compiler_params=pltpu.CompilerParams(vmem_limit_bytes=24 * 2**20),
        name="act",
    )(where, ids, valid, parts, bias)


TURNS = ((0, 0), (1, 3), (3, 1), (2, 2))


def down_kernel(turn, outs, where, ids, act, weight, *rest):
    (keep, *send), wide = rest[-1 - outs : -1], rest[-1]
    c, x, high = where[1], where[2], where[3]
    k = jnp.where(c == 0, TURNS[turn][0], TURNS[turn][1])
    source = lax.rem(x + NX - k, NX)
    wide[...] = jnp.zeros_like(wide)
    for y in range(NY):
        for g in range(ROW // GROUP):
            group = (y * NX + source) * (ROW // GROUP) + g
            low = y * ROW + g * GROUP
            for s in range(CAP):
                at = pl.multiple_of(ids[group, s] * BLOCK, BLOCK)
                wide[low : low + GROUP, pl.ds(at, BLOCK)] = act[
                    y, g * GROUP : (g + 1) * GROUP, s * BLOCK : (s + 1) * BLOCK
                ]
    value = jnp.dot(wide[...], weight[...], preferred_element_type=F32).astype(BF16)
    value = value.reshape(NY, ROW, PIECE)

    def put(ref):
        for y in range(NY):
            ref[lax.rem(y + NZ - high, NZ)] = value[y]

    if send:
        pl.when(k // 2 == c)(functools.partial(put, keep))
        pl.when(k // 2 != c)(functools.partial(put, send[0]))
    else:
        put(keep)


def down(turn, outs, where, ids, act, weight, before=()):
    return pl.pallas_call(
        functools.partial(down_kernel, turn, outs),
        out_shape=[jax.ShapeDtypeStruct((NZ, ROW, PIECE), BF16)] * outs,
        in_specs=[SMEM, SMEM] + [VMEM] * (2 + len(before)),
        out_specs=[VMEM] * outs,
        scratch_shapes=[pltpu.VMEM((NY * ROW, weight.shape[0]), BF16)],
        input_output_aliases={4 + i: i for i in range(len(before))},
        cost_estimate=pl.CostEstimate(
            flops=2 * NY * ROW * weight.size, bytes_accessed=0, transcendentals=0
        ),
        compiler_params=pltpu.CompilerParams(vmem_limit_bytes=24 * 2**20),
        name="down",
    )(where, ids, act, weight, *before)


def pairs(steps):
    return [(x * NC + c, (x + steps[c]) % NX * NC + c) for x in range(NX) for c in range(NC)]


def body(
    hidden_in, norm_gain, norm_shift, up_weight, up_bias, down_weight, down_bias, active, counts
):
    y, x = lax.axis_index("y"), lax.axis_index("x")
    z, c = lax.axis_index("z"), lax.axis_index("c")
    r, t = y * NX + x, z * NC + c
    odd = lax.rem(r, 2) == 1
    ids, valid = active[:, 0, :], counts[:, 0]
    where = jnp.stack([r, c, x, y]).astype(jnp.int32)
    width = down_bias.shape[0]

    mine = jnp.stack([c, x, c]).astype(jnp.int32)
    others = jnp.stack([1 - c, x, c]).astype(jnp.int32)
    scales = jnp.stack([norm_gain, norm_shift]).astype(F32)
    normed = norm(c.reshape(1), hidden_in, scales)
    own = lax.all_to_all(normed, ("y", "x"), split_axis=0, concat_axis=0, tiled=True)
    other = lax.ppermute(own, "c", around(NC, 1))
    own, other = (v.reshape(NY, NX, GROUP, PIECE) for v in (own, other))
    first = up((0, 1, 2, 3), mine, ids, own, up_weight)
    parts = []
    for turn, before in enumerate(first):
        (part,) = up((turn,), others, ids, other, up_weight, (before,))
        parts.append(part.reshape(NY, ROW, CAP * BLOCK))
    passed = lax.ppermute(parts[0], ("x", "c"), pairs(LEAVES[2]))
    direct = lax.ppermute(parts[1], ("x", "c"), pairs(LEAVES[1]))
    joined = (parts[2].astype(F32) + passed.astype(F32)).astype(BF16)
    joined = lax.ppermute(joined, ("x", "c"), pairs(LEAVES[2]))
    part = (parts[3].astype(F32) + direct.astype(F32) + joined.astype(F32)).astype(BF16)
    part = lax.all_to_all(part, "y", split_axis=0, concat_axis=0, tiled=True)
    bias = up_bias.astype(F32).reshape(-1, BLOCK)
    act = activate(where, ids, valid, part, bias)

    act = lax.all_to_all(act, "y", split_axis=0, concat_axis=0, tiled=True)
    near = lax.ppermute(act, ("x", "c"), pairs(TURNS[1]))
    other_side = lax.ppermute(act, ("x", "c"), pairs(TURNS[2]))
    far = lax.ppermute(near, ("x", "c"), pairs(TURNS[1]))
    even = down(0, 2, where, ids, act, down_weight)
    (odd_keep,) = down(1, 1, where, ids, near, down_weight)
    (odd_send,) = down(2, 1, where, ids, other_side, down_weight)
    odd_got = lax.ppermute(odd_send, "c", around(NC, 1))
    even_keep, even_send = down(3, 2, where, ids, far, down_weight, even)
    even_got = lax.ppermute(even_send, "c", around(NC, 1))
    pair = jnp.stack(
        [
            (kept.astype(F32) + got.astype(F32)).astype(BF16)
            for kept, got in ((even_keep, even_got), (odd_keep, odd_got))
        ],
        axis=1,
    ).reshape(NZ, 2 * ROW, PIECE)
    pair = lax.all_to_all(pair, "z", split_axis=0, concat_axis=0, tiled=True)
    branch = jnp.sum(pair.astype(F32), axis=0).astype(BF16)

    back = [[], []]
    for j, ys, xs, zs, cs in itertools.product(range(2), *map(range, (NY, NX, NZ, NC))):
        row = (zs + ys) % NY * NX + (xs - 2 * cs - j) % NX
        source = ((ys * NX + xs) * NZ + zs) * NC + cs
        back[j].append((source, row * NZ * NC + (ys * NX + xs) // 2))
    first = lax.ppermute(branch[:ROW], ALL, back[0])
    second = lax.ppermute(branch[ROW:], ALL, back[1])
    summed = jnp.concatenate(
        [jnp.where(odd, second, first), jnp.where(odd, first, second)], axis=1
    ).astype(F32)
    resid = lax.dynamic_slice_in_dim(hidden_in, t * width, width, 1).astype(F32)
    return (resid + summed + down_bias.astype(F32)).astype(BF16)


def solution(mesh):
    fine = Mesh(mesh.devices.reshape(NY, NX, NZ, NC), ALL)
    dp, tensor = ("y", "x"), ("z", "c")
    placed = (
        P(dp, None),
        P(),
        P(),
        P(dp, tensor),
        P(tensor),
        P(tensor, dp),
        P(tensor),
        P(None, tensor, None),
        P(None, tensor),
    )
    return jax.shard_map(
        body, mesh=fine, in_specs=placed, out_specs=P(dp, tensor), check_vma=False
    )
```

```python
import functools
import itertools

import jax
import jax.numpy as jnp
from jax import lax
from jax.experimental import pallas as pl
from jax.experimental.pallas import tpu as pltpu
from jax.sharding import Mesh, PartitionSpec as P

BLOCK = 128
GROUP = 32
CAP = 4
GROUPS = 64
NY, NX, NZ, NC = 8, 4, 8, 2
ROW = 64
PIECE = 384
F32 = jnp.float32
BF16 = jnp.bfloat16
ALL = ("y", "x", "z", "c")


def around(size, k):
    return [(i, (i + k) % size) for i in range(size)]


SMEM = pl.BlockSpec(memory_space=pltpu.SMEM)
VMEM = pl.BlockSpec(memory_space=pltpu.VMEM)


def norm_kernel(hidden, scales, out):
    rows, features = hidden.shape
    pieces = features // PIECE

    def piece(p):
        return hidden[:, p * PIECE : (p + 1) * PIECE].astype(F32)

    total = jnp.zeros((rows, PIECE), F32)
    for p in range(pieces):
        total += piece(p)
    mean = jnp.sum(total, axis=1, keepdims=True) / features
    total = jnp.zeros((rows, PIECE), F32)
    for p in range(pieces):
        center = piece(p) - mean
        total += center * center
    spread = jnp.sum(total, axis=1, keepdims=True) / features
    scale = lax.rsqrt(spread + 1e-05)
    for p in range(pieces):
        at = slice(p * PIECE, (p + 1) * PIECE)
        value = (piece(p) - mean) * scale * scales[0:1, at] + scales[1:2, at]
        out[p] = value.astype(BF16)


def norm(hidden, scales):
    features = hidden.shape[1]
    pieces = features // PIECE
    return pl.pallas_call(
        norm_kernel,
        out_shape=jax.ShapeDtypeStruct((pieces, GROUP, PIECE), BF16),
        in_specs=[VMEM, VMEM],
        out_specs=VMEM,
        compiler_params=pltpu.CompilerParams(vmem_limit_bytes=32 * 2**20),
        name="norm",
    )(hidden, scales)


LEAVES = ((2, 2), (3, 1), (1, 3), (0, 0))


def up_kernel(turns, at, ids, rows, weight, *rest):
    total = rest[-1]
    outs = rest[-1 - len(turns) : -1]
    h, x, c = at[0], at[1], at[2]
    for turn, out in zip(turns, outs):
        k = jnp.where(c == 0, LEAVES[turn][0], LEAVES[turn][1])
        target = lax.rem(x + k, NX)
        block_rows = rows[:, target].reshape(NY * GROUP, PIECE)
        total[...] = jnp.dot(block_rows, weight[...], preferred_element_type=F32)
        for y in range(NY):
            group = (y * NX + target) * (ROW // GROUP) + h
            for s in range(CAP):
                block = pl.multiple_of(ids[s * GROUPS + group] * BLOCK, BLOCK)
                picked = total[y * GROUP : (y + 1) * GROUP, pl.ds(block, BLOCK)]
                out[y, h, :, s * BLOCK : (s + 1) * BLOCK] = picked.astype(BF16)


def up(turns, at, ids, rows, weight, before=()):
    shape = jax.ShapeDtypeStruct((NY, ROW // GROUP, GROUP, CAP * BLOCK), BF16)
    return pl.pallas_call(
        functools.partial(up_kernel, turns),
        out_shape=[shape] * len(turns),
        in_specs=[SMEM, SMEM, VMEM, VMEM] + [VMEM] * len(before),
        out_specs=[VMEM] * len(turns),
        scratch_shapes=[pltpu.VMEM((NY * GROUP, weight.shape[1]), F32)],
        input_output_aliases={4 + i: i for i in range(len(before))},
        cost_estimate=pl.CostEstimate(
            flops=2 * len(turns) * NY * GROUP * weight.size,
            bytes_accessed=0,
            transcendentals=0,
        ),
        compiler_params=pltpu.CompilerParams(vmem_limit_bytes=24 * 2**20),
        name="up_second" if before else "up_first",
    )(at, ids, rows, weight, *before)


def act_kernel(where, ids, valid, parts, bias, out):
    pre = jnp.sum(parts[...].astype(F32), axis=0)
    for g in range(ROW // GROUP):
        group = where[0] * (ROW // GROUP) + g
        for s in range(CAP):
            block = ids[s * GROUPS + group]
            keep = (s < valid[group]).astype(F32)
            mine = pre[g * GROUP : (g + 1) * GROUP, s * BLOCK : (s + 1) * BLOCK]
            value = (jnp.maximum(mine + bias[pl.ds(block, 1), :], 0.0) * keep).astype(BF16)
            for copy in range(out.shape[0]):
                out[copy, g * GROUP : (g + 1) * GROUP, s * BLOCK : (s + 1) * BLOCK] = value


def activate(where, ids, valid, parts, bias):
    return pl.pallas_call(
        act_kernel,
        out_shape=jax.ShapeDtypeStruct((NY, ROW, CAP * BLOCK), BF16),
        in_specs=[SMEM, SMEM, SMEM, VMEM, VMEM],
        out_specs=VMEM,
        compiler_params=pltpu.CompilerParams(vmem_limit_bytes=24 * 2**20),
        name="act",
    )(where, ids, valid, parts, bias)


TURNS = ((0, 0), (1, 3), (3, 1), (2, 2))


def down_kernel(turn, outs, where, ids, act, weight, *rest):
    (keep, *send), wide = rest[-1 - outs : -1], rest[-1]
    c, x, high = where[1], where[2], where[3]
    k = jnp.where(c == 0, TURNS[turn][0], TURNS[turn][1])
    source = lax.rem(x + NX - k, NX)
    wide[...] = jnp.zeros_like(wide)
    for y in range(NY):
        for g in range(ROW // GROUP):
            group = (y * NX + source) * (ROW // GROUP) + g
            low = y * ROW + g * GROUP
            for s in range(CAP):
                at = pl.multiple_of(ids[s * GROUPS + group] * BLOCK, BLOCK)
                wide[low : low + GROUP, pl.ds(at, BLOCK)] = act[
                    y, g * GROUP : (g + 1) * GROUP, s * BLOCK : (s + 1) * BLOCK
                ]
    value = jnp.dot(wide[...], weight[...], preferred_element_type=F32).astype(BF16)
    value = value.reshape(NY, ROW, PIECE)

    def put(ref):
        for y in range(NY):
            ref[lax.rem(y + NZ - high, NZ)] = value[y]

    if send:
        pl.when(k // 2 == c)(functools.partial(put, keep))
        pl.when(k // 2 != c)(functools.partial(put, send[0]))
    else:
        put(keep)


def down(turn, outs, where, ids, act, weight, before=()):
    return pl.pallas_call(
        functools.partial(down_kernel, turn, outs),
        out_shape=[jax.ShapeDtypeStruct((NZ, ROW, PIECE), BF16)] * outs,
        in_specs=[SMEM, SMEM] + [VMEM] * (2 + len(before)),
        out_specs=[VMEM] * outs,
        scratch_shapes=[pltpu.VMEM((NY * ROW, weight.shape[0]), BF16)],
        input_output_aliases={4 + i: i for i in range(len(before))},
        cost_estimate=pl.CostEstimate(
            flops=2 * NY * ROW * weight.size, bytes_accessed=0, transcendentals=0
        ),
        compiler_params=pltpu.CompilerParams(vmem_limit_bytes=24 * 2**20),
        name="down",
    )(where, ids, act, weight, *before)


def pairs(steps):
    return [(x * NC + c, (x + steps[c]) % NX * NC + c) for x in range(NX) for c in range(NC)]


def body(
    hidden_in, norm_gain, norm_shift, up_weight, up_bias, down_weight, down_bias, active, counts
):
    y, x = lax.axis_index("y"), lax.axis_index("x")
    z, c = lax.axis_index("z"), lax.axis_index("c")
    r, t = y * NX + x, z * NC + c
    odd = lax.rem(r, 2) == 1
    ids, valid = active[:, 0, :].T.reshape(-1), counts.reshape(-1)
    where = jnp.stack([r, c, x, y]).astype(jnp.int32)
    width = down_bias.shape[0]

    mine = jnp.stack([c, x, c]).astype(jnp.int32)
    others = jnp.stack([1 - c, x, c]).astype(jnp.int32)
    scales = jnp.stack([norm_gain, norm_shift]).astype(F32)
    normed = norm(lax.dynamic_slice_in_dim(hidden_in, c * GROUP, GROUP, 0), scales)
    own = lax.all_to_all(normed, ("y", "x"), split_axis=0, concat_axis=0, tiled=True)
    other = lax.ppermute(own, "c", around(NC, 1))
    own, other = (v.reshape(NY, NX, GROUP, PIECE) for v in (own, other))
    first = up((0, 1, 2, 3), mine, ids, own, up_weight)
    parts = []
    for turn, before in enumerate(first):
        (part,) = up((turn,), others, ids, other, up_weight, (before,))
        parts.append(part.reshape(NY, ROW, CAP * BLOCK))
    passed = lax.ppermute(parts[0], ("x", "c"), pairs(LEAVES[2]))
    direct = lax.ppermute(parts[1], ("x", "c"), pairs(LEAVES[1]))
    joined = (parts[2].astype(F32) + passed.astype(F32)).astype(BF16)
    joined = lax.ppermute(joined, ("x", "c"), pairs(LEAVES[2]))
    part = (parts[3].astype(F32) + direct.astype(F32) + joined.astype(F32)).astype(BF16)
    part = lax.all_to_all(part, "y", split_axis=0, concat_axis=0, tiled=True)
    bias = up_bias.astype(F32).reshape(-1, BLOCK)
    act = activate(where, ids, valid, part, bias)

    act = lax.all_to_all(act, "y", split_axis=0, concat_axis=0, tiled=True)
    near = lax.ppermute(act, ("x", "c"), pairs(TURNS[1]))
    other_side = lax.ppermute(act, ("x", "c"), pairs(TURNS[2]))
    even = down(0, 2, where, ids, act, down_weight)
    near, even = lax.optimization_barrier((near, even))
    far = lax.ppermute(near, ("x", "c"), pairs(TURNS[1]))
    (odd_keep,) = down(1, 1, where, ids, near, down_weight)
    (odd_send,) = down(2, 1, where, ids, other_side, down_weight)
    odd_got = lax.ppermute(odd_send, "c", around(NC, 1))
    even_keep, even_send = down(3, 2, where, ids, far, down_weight, even)
    even_got = lax.ppermute(even_send, "c", around(NC, 1))
    pair = jnp.stack(
        [
            (kept.astype(F32) + got.astype(F32)).astype(BF16)
            for kept, got in ((even_keep, even_got), (odd_keep, odd_got))
        ],
        axis=1,
    ).reshape(NZ, 2 * ROW, PIECE)
    pair = lax.all_to_all(pair, "z", split_axis=0, concat_axis=0, tiled=True)
    branch = jnp.sum(pair.astype(F32), axis=0).astype(BF16)

    back = [[], []]
    for j, ys, xs, zs, cs in itertools.product(range(2), *map(range, (NY, NX, NZ, NC))):
        row = (zs + ys) % NY * NX + (xs - 2 * cs - j) % NX
        source = ((ys * NX + xs) * NZ + zs) * NC + cs
        back[j].append((source, row * NZ * NC + (ys * NX + xs) // 2))
    first = lax.ppermute(branch[:ROW], ALL, back[0])
    second = lax.ppermute(branch[ROW:], ALL, back[1])
    summed = jnp.concatenate(
        [jnp.where(odd, second, first), jnp.where(odd, first, second)], axis=1
    ).astype(F32)
    resid = lax.dynamic_slice_in_dim(hidden_in, t * width, width, 1).astype(F32)
    return (resid + summed + down_bias.astype(F32)).astype(BF16)


def solution(mesh):
    fine = Mesh(mesh.devices.reshape(NY, NX, NZ, NC), ALL)
    dp, tensor = ("y", "x"), ("z", "c")
    placed = (
        P(dp, None),
        P(),
        P(),
        P(dp, tensor),
        P(tensor),
        P(tensor, dp),
        P(tensor),
        P(None, tensor, None),
        P(None, tensor),
    )
    return jax.shard_map(
        body, mesh=fine, in_specs=placed, out_specs=P(dp, tensor), check_vma=False
    )
```

```python
import functools
import itertools

import jax
import jax.numpy as jnp
from jax import lax
from jax.experimental import pallas as pl
from jax.experimental.pallas import tpu as pltpu
from jax.sharding import Mesh, PartitionSpec as P

BLOCK = 128
GROUP = 32
CAP = 4
GROUPS = 64
NY, NX, NZ, NC = 8, 4, 8, 2
ROW = 64
PIECE = 384
F32 = jnp.float32
BF16 = jnp.bfloat16
ALL = ("y", "x", "z", "c")


def around(size, k):
    return [(i, (i + k) % size) for i in range(size)]


SMEM = pl.BlockSpec(memory_space=pltpu.SMEM)
VMEM = pl.BlockSpec(memory_space=pltpu.VMEM)


def norm_kernel(hidden, scales, out):
    rows, features = hidden.shape
    pieces = features // PIECE

    def piece(p):
        return hidden[:, p * PIECE : (p + 1) * PIECE].astype(F32)

    total = jnp.zeros((rows, PIECE), F32)
    for p in range(pieces):
        total += piece(p)
    mean = jnp.sum(total, axis=1, keepdims=True) / features
    total = jnp.zeros((rows, PIECE), F32)
    for p in range(pieces):
        center = piece(p) - mean
        total += center * center
    spread = jnp.sum(total, axis=1, keepdims=True) / features
    scale = lax.rsqrt(spread + 1e-05)
    for p in range(pieces):
        at = slice(p * PIECE, (p + 1) * PIECE)
        value = (piece(p) - mean) * scale * scales[0:1, at] + scales[1:2, at]
        out[p] = value.astype(BF16)


def norm(hidden, scales):
    features = hidden.shape[1]
    pieces = features // PIECE
    return pl.pallas_call(
        norm_kernel,
        out_shape=jax.ShapeDtypeStruct((pieces, GROUP, PIECE), BF16),
        in_specs=[VMEM, VMEM],
        out_specs=VMEM,
        compiler_params=pltpu.CompilerParams(vmem_limit_bytes=32 * 2**20),
        name="norm",
    )(hidden, scales)


LEAVES = ((2, 2), (3, 1), (1, 3), (0, 0))


def up_kernel(turns, at, ids, rows, weight, *rest):
    total = rest[-1]
    outs = rest[-1 - len(turns) : -1]
    h, x, c = at[0], at[1], at[2]
    for turn, out in zip(turns, outs):
        k = jnp.where(c == 0, LEAVES[turn][0], LEAVES[turn][1])
        target = lax.rem(x + k, NX)
        block_rows = rows[:, target].reshape(NY * GROUP, PIECE)
        total[...] = jnp.dot(block_rows, weight[...], preferred_element_type=F32)
        for y in range(NY):
            group = (y * NX + target) * (ROW // GROUP) + h
            for s in range(CAP):
                block = pl.multiple_of(ids[s * GROUPS + group] * BLOCK, BLOCK)
                picked = total[y * GROUP : (y + 1) * GROUP, pl.ds(block, BLOCK)]
                out[y, h, :, s * BLOCK : (s + 1) * BLOCK] = picked.astype(BF16)


def up(turns, at, ids, rows, weight, before=()):
    shape = jax.ShapeDtypeStruct((NY, ROW // GROUP, GROUP, CAP * BLOCK), BF16)
    return pl.pallas_call(
        functools.partial(up_kernel, turns),
        out_shape=[shape] * len(turns),
        in_specs=[SMEM, SMEM, VMEM, VMEM] + [VMEM] * len(before),
        out_specs=[VMEM] * len(turns),
        scratch_shapes=[pltpu.VMEM((NY * GROUP, weight.shape[1]), F32)],
        input_output_aliases={4 + i: i for i in range(len(before))},
        cost_estimate=pl.CostEstimate(
            flops=2 * len(turns) * NY * GROUP * weight.size,
            bytes_accessed=0,
            transcendentals=0,
        ),
        compiler_params=pltpu.CompilerParams(vmem_limit_bytes=24 * 2**20),
        name="up_second" if before else "up_first",
    )(at, ids, rows, weight, *before)


def act_kernel(where, ids, valid, parts, bias, out):
    pre = jnp.sum(parts[...].astype(F32), axis=0)
    for g in range(ROW // GROUP):
        group = where[0] * (ROW // GROUP) + g
        for s in range(CAP):
            block = ids[s * GROUPS + group]
            keep = (s < valid[group]).astype(F32)
            mine = pre[g * GROUP : (g + 1) * GROUP, s * BLOCK : (s + 1) * BLOCK]
            value = (jnp.maximum(mine + bias[pl.ds(block, 1), :], 0.0) * keep).astype(BF16)
            for copy in range(out.shape[0]):
                out[copy, g * GROUP : (g + 1) * GROUP, s * BLOCK : (s + 1) * BLOCK] = value


def activate(where, ids, valid, parts, bias):
    return pl.pallas_call(
        act_kernel,
        out_shape=jax.ShapeDtypeStruct((NY, ROW, CAP * BLOCK), BF16),
        in_specs=[SMEM, SMEM, SMEM, VMEM, VMEM],
        out_specs=VMEM,
        compiler_params=pltpu.CompilerParams(vmem_limit_bytes=24 * 2**20),
        name="act",
    )(where, ids, valid, parts, bias)


TURNS = ((0, 0), (1, 3), (3, 1), (2, 2))


def down_kernel(turn, outs, where, ids, act, weight, *rest):
    (keep, *send), wide = rest[-1 - outs : -1], rest[-1]
    c, x, high = where[1], where[2], where[3]
    k = jnp.where(c == 0, TURNS[turn][0], TURNS[turn][1])
    source = lax.rem(x + NX - k, NX)
    wide[...] = jnp.zeros_like(wide)
    for y in range(NY):
        for g in range(ROW // GROUP):
            group = (y * NX + source) * (ROW // GROUP) + g
            low = y * ROW + g * GROUP
            for s in range(CAP):
                at = pl.multiple_of(ids[s * GROUPS + group] * BLOCK, BLOCK)
                wide[low : low + GROUP, pl.ds(at, BLOCK)] = act[
                    y, g * GROUP : (g + 1) * GROUP, s * BLOCK : (s + 1) * BLOCK
                ]
    value = jnp.dot(wide[...], weight[...], preferred_element_type=F32).astype(BF16)
    value = value.reshape(NY, ROW, PIECE)

    def put(ref):
        for y in range(NY):
            ref[lax.rem(y + NZ - high, NZ)] = value[y]

    if send:
        pl.when(k // 2 == c)(functools.partial(put, keep))
        pl.when(k // 2 != c)(functools.partial(put, send[0]))
    else:
        put(keep)


def down(turn, outs, where, ids, act, weight, before=()):
    return pl.pallas_call(
        functools.partial(down_kernel, turn, outs),
        out_shape=[jax.ShapeDtypeStruct((NZ, ROW, PIECE), BF16)] * outs,
        in_specs=[SMEM, SMEM] + [VMEM] * (2 + len(before)),
        out_specs=[VMEM] * outs,
        scratch_shapes=[pltpu.VMEM((NY * ROW, weight.shape[0]), BF16)],
        input_output_aliases={4 + i: i for i in range(len(before))},
        cost_estimate=pl.CostEstimate(
            flops=2 * NY * ROW * weight.size, bytes_accessed=0, transcendentals=0
        ),
        compiler_params=pltpu.CompilerParams(vmem_limit_bytes=24 * 2**20),
        name="down",
    )(where, ids, act, weight, *before)


def pairs(steps):
    return [(x * NC + c, (x + steps[c]) % NX * NC + c) for x in range(NX) for c in range(NC)]


def owners_sum(pair):
    parts = lax.all_to_all(pair, "z", split_axis=0, concat_axis=0, tiled=True)
    return jnp.sum(parts.astype(F32), axis=0).astype(BF16)


def body(
    hidden_in, norm_gain, norm_shift, up_weight, up_bias, down_weight, down_bias, active, counts
):
    y, x = lax.axis_index("y"), lax.axis_index("x")
    z, c = lax.axis_index("z"), lax.axis_index("c")
    r, t = y * NX + x, z * NC + c
    odd = lax.rem(r, 2) == 1
    ids, valid = active[:, 0, :].T.reshape(-1), counts.reshape(-1)
    where = jnp.stack([r, c, x, y]).astype(jnp.int32)
    width = down_bias.shape[0]

    mine = jnp.stack([c, x, c]).astype(jnp.int32)
    others = jnp.stack([1 - c, x, c]).astype(jnp.int32)
    scales = jnp.stack([norm_gain, norm_shift]).astype(F32)
    normed = norm(lax.dynamic_slice_in_dim(hidden_in, c * GROUP, GROUP, 0), scales)
    own = lax.all_to_all(normed, ("y", "x"), split_axis=0, concat_axis=0, tiled=True)
    other = lax.ppermute(own, "c", around(NC, 1))
    own, other = (v.reshape(NY, NX, GROUP, PIECE) for v in (own, other))
    first = up((0, 1, 2, 3), mine, ids, own, up_weight)
    parts = []
    for turn, before in enumerate(first):
        (part,) = up((turn,), others, ids, other, up_weight, (before,))
        parts.append(part.reshape(NY, ROW, CAP * BLOCK))
    passed = lax.ppermute(parts[0], ("x", "c"), pairs(LEAVES[2]))
    direct = lax.ppermute(parts[1], ("x", "c"), pairs(LEAVES[1]))
    joined = (parts[2].astype(F32) + passed.astype(F32)).astype(BF16)
    joined = lax.ppermute(joined, ("x", "c"), pairs(LEAVES[2]))
    part = (parts[3].astype(F32) + direct.astype(F32) + joined.astype(F32)).astype(BF16)
    part = lax.all_to_all(part, "y", split_axis=0, concat_axis=0, tiled=True)
    bias = up_bias.astype(F32).reshape(-1, BLOCK)
    act = activate(where, ids, valid, part, bias)

    act = lax.all_to_all(act, "y", split_axis=0, concat_axis=0, tiled=True)
    near = lax.ppermute(act, ("x", "c"), pairs(TURNS[1]))
    other_side = lax.ppermute(act, ("x", "c"), pairs(TURNS[2]))
    even = down(0, 2, where, ids, act, down_weight)
    near, even = lax.optimization_barrier((near, even))
    far = lax.ppermute(near, ("x", "c"), pairs(TURNS[1]))
    (odd_keep,) = down(1, 1, where, ids, near, down_weight)
    (odd_send,) = down(2, 1, where, ids, other_side, down_weight)
    odd_got = lax.ppermute(odd_send, "c", around(NC, 1))
    odd_pair = (odd_keep.astype(F32) + odd_got.astype(F32)).astype(BF16)
    even, odd_pair = lax.optimization_barrier((even, odd_pair))
    odd_branch = owners_sum(odd_pair)
    even_keep, even_send = down(3, 2, where, ids, far, down_weight, even)
    even_got = lax.ppermute(even_send, "c", around(NC, 1))
    even_branch = owners_sum((even_keep.astype(F32) + even_got.astype(F32)).astype(BF16))

    back = [[], []]
    for j, ys, xs, zs, cs in itertools.product(range(2), *map(range, (NY, NX, NZ, NC))):
        row = (zs + ys) % NY * NX + (xs - 2 * cs - j) % NX
        source = ((ys * NX + xs) * NZ + zs) * NC + cs
        back[j].append((source, row * NZ * NC + (ys * NX + xs) // 2))
    first = lax.ppermute(even_branch, ALL, back[0])
    second = lax.ppermute(odd_branch, ALL, back[1])
    summed = jnp.concatenate(
        [jnp.where(odd, second, first), jnp.where(odd, first, second)], axis=1
    ).astype(F32)
    resid = lax.dynamic_slice_in_dim(hidden_in, t * width, width, 1).astype(F32)
    return (resid + summed + down_bias.astype(F32)).astype(BF16)


def solution(mesh):
    fine = Mesh(mesh.devices.reshape(NY, NX, NZ, NC), ALL)
    dp, tensor = ("y", "x"), ("z", "c")
    placed = (
        P(dp, None),
        P(),
        P(),
        P(dp, tensor),
        P(tensor),
        P(tensor, dp),
        P(tensor),
        P(None, tensor, None),
        P(None, tensor),
    )
    return jax.shard_map(
        body, mesh=fine, in_specs=placed, out_specs=P(dp, tensor), check_vma=False
    )
```

```python
import functools
import itertools

import jax
import jax.numpy as jnp
from jax import lax
from jax.experimental import pallas as pl
from jax.experimental.pallas import tpu as pltpu
from jax.sharding import Mesh, PartitionSpec as P

BLOCK = 128
GROUP = 32
CAP = 4
GROUPS = 64
NY, NX, NZ, NC = 8, 4, 8, 2
ROW = 64
PIECE = 384
F32 = jnp.float32
BF16 = jnp.bfloat16
ALL = ("y", "x", "z", "c")


def around(size, k):
    return [(i, (i + k) % size) for i in range(size)]


SMEM = pl.BlockSpec(memory_space=pltpu.SMEM)
VMEM = pl.BlockSpec(memory_space=pltpu.VMEM)


def norm_kernel(hidden, scales, out):
    rows, features = hidden.shape
    pieces = features // PIECE
    gains = scales[:features].astype(F32).reshape(1, features)
    shifts = scales[features:].astype(F32).reshape(1, features)

    def piece(p):
        return hidden[:, p * PIECE : (p + 1) * PIECE].astype(F32)

    total = jnp.zeros((rows, PIECE), F32)
    for p in range(pieces):
        total += piece(p)
    mean = jnp.sum(total, axis=1, keepdims=True) / features
    total = jnp.zeros((rows, PIECE), F32)
    for p in range(pieces):
        center = piece(p) - mean
        total += center * center
    spread = jnp.sum(total, axis=1, keepdims=True) / features
    scale = lax.rsqrt(spread + 1e-05)
    for p in range(pieces):
        at = slice(p * PIECE, (p + 1) * PIECE)
        value = (piece(p) - mean) * scale * gains[:, at] + shifts[:, at]
        out[p] = value.astype(BF16)


def norm(hidden, scales):
    features = hidden.shape[1]
    pieces = features // PIECE
    return pl.pallas_call(
        norm_kernel,
        out_shape=jax.ShapeDtypeStruct((pieces, GROUP, PIECE), BF16),
        in_specs=[VMEM, VMEM],
        out_specs=VMEM,
        compiler_params=pltpu.CompilerParams(vmem_limit_bytes=32 * 2**20),
        name="norm",
    )(hidden, scales)


LEAVES = ((2, 2), (3, 1), (1, 3), (0, 0))


def up_kernel(turns, at, ids, rows, weight, *rest):
    total = rest[-1]
    outs = rest[-1 - len(turns) : -1]
    h, x, c = at[0], at[1], at[2]
    for turn, out in zip(turns, outs):
        k = jnp.where(c == 0, LEAVES[turn][0], LEAVES[turn][1])
        target = lax.rem(x + k, NX)
        block_rows = rows[:, target].reshape(NY * GROUP, PIECE)
        total[...] = jnp.dot(block_rows, weight[...], preferred_element_type=F32)
        for y in range(NY):
            group = (y * NX + target) * (ROW // GROUP) + h
            for s in range(CAP):
                block = pl.multiple_of(ids[s * GROUPS + group] * BLOCK, BLOCK)
                picked = total[y * GROUP : (y + 1) * GROUP, pl.ds(block, BLOCK)]
                out[y, h, :, s * BLOCK : (s + 1) * BLOCK] = picked.astype(BF16)


def up(turns, at, ids, rows, weight, before=()):
    shape = jax.ShapeDtypeStruct((NY, ROW // GROUP, GROUP, CAP * BLOCK), BF16)
    return pl.pallas_call(
        functools.partial(up_kernel, turns),
        out_shape=[shape] * len(turns),
        in_specs=[SMEM, SMEM, VMEM, VMEM] + [VMEM] * len(before),
        out_specs=[VMEM] * len(turns),
        scratch_shapes=[pltpu.VMEM((NY * GROUP, weight.shape[1]), F32)],
        input_output_aliases={4 + i: i for i in range(len(before))},
        cost_estimate=pl.CostEstimate(
            flops=2 * len(turns) * NY * GROUP * weight.size,
            bytes_accessed=0,
            transcendentals=0,
        ),
        compiler_params=pltpu.CompilerParams(vmem_limit_bytes=24 * 2**20),
        name="up_second" if before else "up_first",
    )(at, ids, rows, weight, *before)


def act_kernel(where, ids, valid, parts, bias, out):
    pre = jnp.sum(parts[...].astype(F32), axis=0)
    for g in range(ROW // GROUP):
        group = where[0] * (ROW // GROUP) + g
        for s in range(CAP):
            block = ids[s * GROUPS + group]
            keep = (s < valid[group]).astype(F32)
            mine = pre[g * GROUP : (g + 1) * GROUP, s * BLOCK : (s + 1) * BLOCK]
            value = (jnp.maximum(mine + bias[pl.ds(block, 1), :], 0.0) * keep).astype(BF16)
            for copy in range(out.shape[0]):
                out[copy, g * GROUP : (g + 1) * GROUP, s * BLOCK : (s + 1) * BLOCK] = value


def activate(where, ids, valid, parts, bias):
    return pl.pallas_call(
        act_kernel,
        out_shape=jax.ShapeDtypeStruct((NY, ROW, CAP * BLOCK), BF16),
        in_specs=[SMEM, SMEM, SMEM, VMEM, VMEM],
        out_specs=VMEM,
        compiler_params=pltpu.CompilerParams(vmem_limit_bytes=24 * 2**20),
        name="act",
    )(where, ids, valid, parts, bias)


TURNS = ((0, 0), (1, 3), (3, 1), (2, 2))


def down_kernel(turn, outs, where, ids, act, weight, *rest):
    (keep, *send), wide = rest[-1 - outs : -1], rest[-1]
    c, x, high = where[1], where[2], where[3]
    k = jnp.where(c == 0, TURNS[turn][0], TURNS[turn][1])
    source = lax.rem(x + NX - k, NX)
    wide[...] = jnp.zeros_like(wide)
    for y in range(NY):
        for g in range(ROW // GROUP):
            group = (y * NX + source) * (ROW // GROUP) + g
            low = y * ROW + g * GROUP
            for s in range(CAP):
                at = pl.multiple_of(ids[s * GROUPS + group] * BLOCK, BLOCK)
                wide[low : low + GROUP, pl.ds(at, BLOCK)] = act[
                    y, g * GROUP : (g + 1) * GROUP, s * BLOCK : (s + 1) * BLOCK
                ]
    value = jnp.dot(wide[...], weight[...], preferred_element_type=F32).astype(BF16)
    value = value.reshape(NY, ROW, PIECE)

    def put(ref):
        for y in range(NY):
            ref[lax.rem(y + NZ - high, NZ)] = value[y]

    if send:
        pl.when(k // 2 == c)(functools.partial(put, keep))
        pl.when(k // 2 != c)(functools.partial(put, send[0]))
    else:
        put(keep)


def down(turn, outs, where, ids, act, weight, before=()):
    return pl.pallas_call(
        functools.partial(down_kernel, turn, outs),
        out_shape=[jax.ShapeDtypeStruct((NZ, ROW, PIECE), BF16)] * outs,
        in_specs=[SMEM, SMEM] + [VMEM] * (2 + len(before)),
        out_specs=[VMEM] * outs,
        scratch_shapes=[pltpu.VMEM((NY * ROW, weight.shape[0]), BF16)],
        input_output_aliases={4 + i: i for i in range(len(before))},
        cost_estimate=pl.CostEstimate(
            flops=2 * NY * ROW * weight.size, bytes_accessed=0, transcendentals=0
        ),
        compiler_params=pltpu.CompilerParams(vmem_limit_bytes=24 * 2**20),
        name="down",
    )(where, ids, act, weight, *before)


def pairs(steps):
    return [(x * NC + c, (x + steps[c]) % NX * NC + c) for x in range(NX) for c in range(NC)]


def body(
    hidden_in, norm_gain, norm_shift, up_weight, up_bias, down_weight, down_bias, active, counts
):
    y, x = lax.axis_index("y"), lax.axis_index("x")
    z, c = lax.axis_index("z"), lax.axis_index("c")
    r, t = y * NX + x, z * NC + c
    odd = lax.rem(r, 2) == 1
    ids, valid = active[:, 0, :].T.reshape(-1), counts.reshape(-1)
    where = jnp.stack([r, c, x, y]).astype(jnp.int32)
    width = down_bias.shape[0]

    mine = jnp.stack([c, x, c]).astype(jnp.int32)
    others = jnp.stack([1 - c, x, c]).astype(jnp.int32)
    scales = jnp.concatenate([norm_gain, norm_shift])
    normed = norm(lax.dynamic_slice_in_dim(hidden_in, c * GROUP, GROUP, 0), scales)
    own = lax.all_to_all(normed, ("y", "x"), split_axis=0, concat_axis=0, tiled=True)
    other = lax.ppermute(own, "c", around(NC, 1))
    own, other = (v.reshape(NY, NX, GROUP, PIECE) for v in (own, other))
    first = up((0, 1, 2, 3), mine, ids, own, up_weight)
    parts = []
    for turn, before in enumerate(first):
        (part,) = up((turn,), others, ids, other, up_weight, (before,))
        parts.append(part.reshape(NY, ROW, CAP * BLOCK))
    passed = lax.ppermute(parts[0], ("x", "c"), pairs(LEAVES[2]))
    direct = lax.ppermute(parts[1], ("x", "c"), pairs(LEAVES[1]))
    joined = (parts[2].astype(F32) + passed.astype(F32)).astype(BF16)
    joined = lax.ppermute(joined, ("x", "c"), pairs(LEAVES[2]))
    part = (parts[3].astype(F32) + direct.astype(F32) + joined.astype(F32)).astype(BF16)
    part = lax.all_to_all(part, "y", split_axis=0, concat_axis=0, tiled=True)
    bias = up_bias.astype(F32).reshape(-1, BLOCK)
    act = activate(where, ids, valid, part, bias)

    act = lax.all_to_all(act, "y", split_axis=0, concat_axis=0, tiled=True)
    near = lax.ppermute(act, ("x", "c"), pairs(TURNS[1]))
    other_side = lax.ppermute(act, ("x", "c"), pairs(TURNS[2]))
    even = down(0, 2, where, ids, act, down_weight)
    near, even = lax.optimization_barrier((near, even))
    far = lax.ppermute(near, ("x", "c"), pairs(TURNS[1]))
    (odd_keep,) = down(1, 1, where, ids, near, down_weight)
    (odd_send,) = down(2, 1, where, ids, other_side, down_weight)
    odd_got = lax.ppermute(odd_send, "c", around(NC, 1))
    even_keep, even_send = down(3, 2, where, ids, far, down_weight, even)
    even_got = lax.ppermute(even_send, "c", around(NC, 1))
    pair = jnp.stack(
        [
            (kept.astype(F32) + got.astype(F32)).astype(BF16)
            for kept, got in ((even_keep, even_got), (odd_keep, odd_got))
        ],
        axis=1,
    ).reshape(NZ, 2 * ROW, PIECE)
    pair = lax.all_to_all(pair, "z", split_axis=0, concat_axis=0, tiled=True)
    branch = jnp.sum(pair.astype(F32), axis=0).astype(BF16)

    resid = lax.dynamic_slice_in_dim(hidden_in, t * width, width, 1).astype(F32)
    base, branch = lax.optimization_barrier((resid + down_bias.astype(F32), branch))
    back = [[], []]
    for j, ys, xs, zs, cs in itertools.product(range(2), *map(range, (NY, NX, NZ, NC))):
        row = (zs + ys) % NY * NX + (xs - 2 * cs - j) % NX
        source = ((ys * NX + xs) * NZ + zs) * NC + cs
        back[j].append((source, row * NZ * NC + (ys * NX + xs) // 2))
    first = lax.ppermute(branch[:ROW], ALL, back[0])
    second = lax.ppermute(branch[ROW:], ALL, back[1])
    summed = jnp.concatenate(
        [jnp.where(odd, second, first), jnp.where(odd, first, second)], axis=1
    ).astype(F32)
    return (base + summed).astype(BF16)


def solution(mesh):
    fine = Mesh(mesh.devices.reshape(NY, NX, NZ, NC), ALL)
    dp, tensor = ("y", "x"), ("z", "c")
    placed = (
        P(dp, None),
        P(),
        P(),
        P(dp, tensor),
        P(tensor),
        P(tensor, dp),
        P(tensor),
        P(None, tensor, None),
        P(None, tensor),
    )
    return jax.shard_map(
        body, mesh=fine, in_specs=placed, out_specs=P(dp, tensor), check_vma=False
    )
```

```python
import functools
import itertools

import jax
import jax.numpy as jnp
from jax import lax
from jax.experimental import pallas as pl
from jax.experimental.pallas import tpu as pltpu
from jax.sharding import Mesh, PartitionSpec as P

BLOCK = 128
GROUP = 32
CAP = 4
GROUPS = 64
NY, NX, NZ, NC = 8, 4, 8, 2
ROW = 64
PIECE = 384
F32 = jnp.float32
BF16 = jnp.bfloat16
ALL = ("y", "x", "z", "c")


def around(size, k):
    return [(i, (i + k) % size) for i in range(size)]


SMEM = pl.BlockSpec(memory_space=pltpu.SMEM)
VMEM = pl.BlockSpec(memory_space=pltpu.VMEM)


def norm_kernel(hidden, scales, out):
    rows, features = hidden.shape
    pieces = features // PIECE
    gains = scales[:features].astype(F32).reshape(1, features)
    shifts = scales[features:].astype(F32).reshape(1, features)

    def piece(p):
        return hidden[:, p * PIECE : (p + 1) * PIECE].astype(F32)

    total = jnp.zeros((rows, PIECE), F32)
    for p in range(pieces):
        total += piece(p)
    mean = jnp.sum(total, axis=1, keepdims=True) / features
    total = jnp.zeros((rows, PIECE), F32)
    for p in range(pieces):
        center = piece(p) - mean
        total += center * center
    spread = jnp.sum(total, axis=1, keepdims=True) / features
    scale = lax.rsqrt(spread + 1e-05)
    for p in range(pieces):
        at = slice(p * PIECE, (p + 1) * PIECE)
        value = (piece(p) - mean) * scale * gains[:, at] + shifts[:, at]
        out[p] = value.astype(BF16)


def norm(hidden, scales):
    features = hidden.shape[1]
    pieces = features // PIECE
    return pl.pallas_call(
        norm_kernel,
        out_shape=jax.ShapeDtypeStruct((pieces, GROUP, PIECE), BF16),
        in_specs=[VMEM, VMEM],
        out_specs=VMEM,
        compiler_params=pltpu.CompilerParams(vmem_limit_bytes=32 * 2**20),
        name="norm",
    )(hidden, scales)


LEAVES = ((2, 2), (3, 1), (1, 3), (0, 0))


def up_kernel(turns, at, ids, rows, weight, *rest):
    total = rest[-1]
    outs = rest[-1 - len(turns) : -1]
    h, x, c = at[0], at[1], at[2]
    for turn, out in zip(turns, outs):
        k = jnp.where(c == 0, LEAVES[turn][0], LEAVES[turn][1])
        target = lax.rem(x + k, NX)
        block_rows = rows[:, target].reshape(NY * GROUP, PIECE)
        total[...] = jnp.dot(block_rows, weight[...], preferred_element_type=F32)
        for y in range(NY):
            group = (y * NX + target) * (ROW // GROUP) + h
            for s in range(CAP):
                block = pl.multiple_of(ids[s * GROUPS + group] * BLOCK, BLOCK)
                picked = total[y * GROUP : (y + 1) * GROUP, pl.ds(block, BLOCK)]
                out[y, h, :, s * BLOCK : (s + 1) * BLOCK] = picked.astype(BF16)


def up(turns, at, ids, rows, weight, before=()):
    shape = jax.ShapeDtypeStruct((NY, ROW // GROUP, GROUP, CAP * BLOCK), BF16)
    return pl.pallas_call(
        functools.partial(up_kernel, turns),
        out_shape=[shape] * len(turns),
        in_specs=[SMEM, SMEM, VMEM, VMEM] + [VMEM] * len(before),
        out_specs=[VMEM] * len(turns),
        scratch_shapes=[pltpu.VMEM((NY * GROUP, weight.shape[1]), F32)],
        input_output_aliases={4 + i: i for i in range(len(before))},
        cost_estimate=pl.CostEstimate(
            flops=2 * len(turns) * NY * GROUP * weight.size,
            bytes_accessed=0,
            transcendentals=0,
        ),
        compiler_params=pltpu.CompilerParams(vmem_limit_bytes=24 * 2**20),
        name="up_second" if before else "up_first",
    )(at, ids, rows, weight, *before)


def act_kernel(where, ids, valid, parts, bias, out):
    pre = jnp.sum(parts[...].astype(F32), axis=0)
    for g in range(ROW // GROUP):
        group = where[0] * (ROW // GROUP) + g
        for s in range(CAP):
            block = ids[s * GROUPS + group]
            keep = (s < valid[group]).astype(F32)
            mine = pre[g * GROUP : (g + 1) * GROUP, s * BLOCK : (s + 1) * BLOCK]
            value = (jnp.maximum(mine + bias[pl.ds(block, 1), :], 0.0) * keep).astype(BF16)
            for copy in range(out.shape[0]):
                out[copy, g * GROUP : (g + 1) * GROUP, s * BLOCK : (s + 1) * BLOCK] = value


def activate(where, ids, valid, parts, bias):
    return pl.pallas_call(
        act_kernel,
        out_shape=jax.ShapeDtypeStruct((NY, ROW, CAP * BLOCK), BF16),
        in_specs=[SMEM, SMEM, SMEM, VMEM, VMEM],
        out_specs=VMEM,
        compiler_params=pltpu.CompilerParams(vmem_limit_bytes=24 * 2**20),
        name="act",
    )(where, ids, valid, parts, bias)


TURNS = ((0, 0), (1, 3), (3, 1), (2, 2))


def down_kernel(turn, outs, where, ids, act, weight, *rest):
    (keep, *send), wide = rest[-1 - outs : -1], rest[-1]
    c, x, high = where[1], where[2], where[3]
    k = jnp.where(c == 0, TURNS[turn][0], TURNS[turn][1])
    source = lax.rem(x + NX - k, NX)
    wide[...] = jnp.zeros_like(wide)
    for y in range(NY):
        for g in range(ROW // GROUP):
            group = (y * NX + source) * (ROW // GROUP) + g
            low = y * ROW + g * GROUP
            for s in range(CAP):
                at = pl.multiple_of(ids[s * GROUPS + group] * BLOCK, BLOCK)
                wide[low : low + GROUP, pl.ds(at, BLOCK)] = act[
                    y, g * GROUP : (g + 1) * GROUP, s * BLOCK : (s + 1) * BLOCK
                ]
    value = jnp.dot(wide[...], weight[...], preferred_element_type=F32).astype(BF16)
    value = value.reshape(NY, ROW, PIECE)

    def put(ref):
        for y in range(NY):
            ref[lax.rem(y + NZ - high, NZ)] = value[y]

    if send:
        pl.when(k // 2 == c)(functools.partial(put, keep))
        pl.when(k // 2 != c)(functools.partial(put, send[0]))
    else:
        put(keep)


def down(turn, outs, where, ids, act, weight, before=()):
    return pl.pallas_call(
        functools.partial(down_kernel, turn, outs),
        out_shape=[jax.ShapeDtypeStruct((NZ, ROW, PIECE), BF16)] * outs,
        in_specs=[SMEM, SMEM] + [VMEM] * (2 + len(before)),
        out_specs=[VMEM] * outs,
        scratch_shapes=[pltpu.VMEM((NY * ROW, weight.shape[0]), BF16)],
        input_output_aliases={4 + i: i for i in range(len(before))},
        cost_estimate=pl.CostEstimate(
            flops=2 * NY * ROW * weight.size, bytes_accessed=0, transcendentals=0
        ),
        compiler_params=pltpu.CompilerParams(vmem_limit_bytes=24 * 2**20),
        name="down",
    )(where, ids, act, weight, *before)


def pairs(steps):
    return [(x * NC + c, (x + steps[c]) % NX * NC + c) for x in range(NX) for c in range(NC)]


def body(
    hidden_in, norm_gain, norm_shift, up_weight, up_bias, down_weight, down_bias, active, counts
):
    y, x = lax.axis_index("y"), lax.axis_index("x")
    z, c = lax.axis_index("z"), lax.axis_index("c")
    r, t = y * NX + x, z * NC + c
    odd = lax.rem(r, 2) == 1
    ids, valid = active[:, 0, :].T.reshape(-1), counts.reshape(-1)
    where = jnp.stack([r, c, x, y]).astype(jnp.int32)
    width = down_bias.shape[0]

    mine = jnp.stack([c, x, c]).astype(jnp.int32)
    others = jnp.stack([1 - c, x, c]).astype(jnp.int32)
    scales = jnp.concatenate([norm_gain, norm_shift])
    normed = norm(lax.dynamic_slice_in_dim(hidden_in, c * GROUP, GROUP, 0), scales)
    own = lax.all_to_all(normed, ("y", "x"), split_axis=0, concat_axis=0, tiled=True)
    other = lax.ppermute(own, "c", around(NC, 1))
    own, other = (v.reshape(NY, NX, GROUP, PIECE) for v in (own, other))
    first = up((0, 1, 2, 3), mine, ids, own, up_weight)
    parts = []
    for turn, before in enumerate(first):
        (part,) = up((turn,), others, ids, other, up_weight, (before,))
        parts.append(part.reshape(NY, ROW, CAP * BLOCK))
    passed = lax.ppermute(parts[0], ("x", "c"), pairs(LEAVES[2]))
    direct = lax.ppermute(parts[1], ("x", "c"), pairs(LEAVES[1]))
    joined = (parts[2].astype(F32) + passed.astype(F32)).astype(BF16)
    joined = lax.ppermute(joined, ("x", "c"), pairs(LEAVES[2]))
    part = (parts[3].astype(F32) + direct.astype(F32) + joined.astype(F32)).astype(BF16)
    part = lax.all_to_all(part, "y", split_axis=0, concat_axis=0, tiled=True)
    bias = up_bias.astype(F32).reshape(-1, BLOCK)
    resid = lax.dynamic_slice_in_dim(hidden_in, t * width, width, 1).astype(F32)
    base, bias = lax.optimization_barrier((resid + down_bias.astype(F32), bias))
    act = activate(where, ids, valid, part, bias)

    act = lax.all_to_all(act, "y", split_axis=0, concat_axis=0, tiled=True)
    near = lax.ppermute(act, ("x", "c"), pairs(TURNS[1]))
    other_side = lax.ppermute(act, ("x", "c"), pairs(TURNS[2]))
    even = down(0, 2, where, ids, act, down_weight)
    near, even = lax.optimization_barrier((near, even))
    far = lax.ppermute(near, ("x", "c"), pairs(TURNS[1]))
    (odd_keep,) = down(1, 1, where, ids, near, down_weight)
    (odd_send,) = down(2, 1, where, ids, other_side, down_weight)
    odd_got = lax.ppermute(odd_send, "c", around(NC, 1))
    even_keep, even_send = down(3, 2, where, ids, far, down_weight, even)
    even_got = lax.ppermute(even_send, "c", around(NC, 1))
    pair = jnp.stack(
        [
            (kept.astype(F32) + got.astype(F32)).astype(BF16)
            for kept, got in ((even_keep, even_got), (odd_keep, odd_got))
        ],
        axis=1,
    ).reshape(NZ, 2 * ROW, PIECE)
    pair = lax.all_to_all(pair, "z", split_axis=0, concat_axis=0, tiled=True)
    branch = jnp.sum(pair.astype(F32), axis=0).astype(BF16)

    back = [[], []]
    for j, ys, xs, zs, cs in itertools.product(range(2), *map(range, (NY, NX, NZ, NC))):
        row = (zs + ys) % NY * NX + (xs - 2 * cs - j) % NX
        source = ((ys * NX + xs) * NZ + zs) * NC + cs
        back[j].append((source, row * NZ * NC + (ys * NX + xs) // 2))
    first = lax.ppermute(branch[:ROW], ALL, back[0])
    second = lax.ppermute(branch[ROW:], ALL, back[1])
    summed = jnp.concatenate(
        [jnp.where(odd, second, first), jnp.where(odd, first, second)], axis=1
    ).astype(F32)
    return (base + summed).astype(BF16)


def solution(mesh):
    fine = Mesh(mesh.devices.reshape(NY, NX, NZ, NC), ALL)
    dp, tensor = ("y", "x"), ("z", "c")
    placed = (
        P(dp, None),
        P(),
        P(),
        P(dp, tensor),
        P(tensor),
        P(tensor, dp),
        P(tensor),
        P(None, tensor, None),
        P(None, tensor),
    )
    return jax.shard_map(
        body, mesh=fine, in_specs=placed, out_specs=P(dp, tensor), check_vma=False
    )
```
